256 devices in a mesh: dp: 32 (over x_hi, z, core), mp: 8 (over y, x_lo).
Axes of the slice: x: 4 (x_hi: 2, x_lo: 2; x = x_hi * 2 + x_lo), y: 4, z: 8, core: 2. Of those that a mesh axis runs over, the one named last changes fastest.
Arguments:
- acts: bfloat16 [32768, 8192], P('dp', 'mp'), may hold values from -6 to 6
- cotangent: bfloat16 [32768, 8, 256], P('dp', 'mp'), may hold values from -0.03125 to 0.03125
- master: float32 [8192, 8, 256], P('dp', 'mp'), may hold values from -0.0625 to 0.0625
- first_moment: float32 [8192, 8, 256], P('dp', 'mp'), may hold values from -6 to 6
- second_moment: float32 [8192, 8, 256], P('dp', 'mp'), may hold values from 0.25 to 4
- long_acts: bfloat16 [8192, 8192], P('dp'), may hold values from -6 to 6
Outputs:
- new_master: float32 [8192, 8, 256], P(('dp', 'mp'))
- new_first: float32 [8192, 8, 256], P(('dp', 'mp'))
- new_second: float32 [8192, 8, 256], P(('dp', 'mp'))
- long_kv: bfloat16 [8192, 8, 256], P('dp', 'mp')
The draws below stay inside these ranges and needn't reach their ends.
All inputs are finite; a program needn't handle non-finite values.
Results may differ from the reference program's by a relative error of at most 0.005.
Values may be sent and summed in bfloat16 or wider, within the bound.
A program may use at most 128 MiB of HBM per device.

```python
import math
import jax
import jax.numpy as jnp

D = 8192
KVH = 8
HD = 128
TOKENS = 32768
LTOKENS = 8192


def block_levels(rng, shape, split, least, top_value):
    loudness = 1.0
    for position, shards_of in split:
        steps = jax.random.uniform(jax.random.fold_in(jax.random.fold_in(rng, 6), position), (shards_of,), jnp.float32, least / len(split), top_value / len(split))
        loudness = loudness * jnp.repeat(jnp.exp(steps), shape[position] // shards_of).reshape((-1,) + (1,) * (len(shape) - 1 - position))
    return loudness


def scatter_about(stream_key, shape, scale, most, split=(), kind=jnp.bfloat16):
    result = jax.random.normal(stream_key, shape, jnp.float32) * scale
    if len(split) > 0:
        result = block_levels(stream_key, shape, split, -0.22, 0.18) * result
    return jnp.clip(result, min=-most, max=most).astype(kind)


def setup_inputs(seed: int = 0) -> dict:
    key_list = jax.random.split(jax.random.key(seed), 7)
    return {
        "acts": scatter_about(key_list[0], (TOKENS, D), 1.0, 6.0, ((0, 32), (1, 8))),
        "cotangent": scatter_about(key_list[1], (TOKENS, KVH, 2 * HD), TOKENS ** -0.5, 0.03125, ((0, 32), (1, 8))),
        "master": scatter_about(key_list[2], (D, KVH, 2 * HD), D ** -0.5, 0.0625, ((0, 32), (1, 8)), jnp.float32),
        "first_moment": scatter_about(key_list[3], (D, KVH, 2 * HD), 1.0, 6.0, ((0, 32), (1, 8)), jnp.float32),
        "second_moment": jnp.clip(jnp.exp(math.log(4.0) - 2.7725887 * jax.random.uniform(key_list[4], (D, KVH, 2 * HD), jnp.float32) ** block_levels(key_list[4], (D, KVH, 2 * HD), ((0, 32), (1, 8)), -0.2, 0.2)), 0.25, 4.0),
        "long_acts": scatter_about(key_list[5], (LTOKENS, D), 1.0, 6.0, ((0, 32),)),
    }


beta_one = 0.9
beta_two = 0.95
learn_rate = 0.001
decay_rate = 0.1
adam_eps = 1e-08
steps_done = 100

def reference(acts, cotangent, master, first_moment, second_moment, long_acts):
    flat_cot = cotangent.reshape(cotangent.shape[0], -1)
    grad = jnp.dot(acts.T, flat_cot, preferred_element_type=jnp.float32).reshape(master.shape)
    new_first = beta_one * first_moment + (1.0 - beta_one) * grad
    new_second = beta_two * second_moment + (1.0 - beta_two) * grad * grad
    fix_one = 1.0 - beta_one ** steps_done
    fix_two = 1.0 - beta_two ** steps_done
    update = new_first / fix_one / (jnp.sqrt(new_second / fix_two) + adam_eps) + decay_rate * master
    new_master = master - learn_rate * update
    weights = new_master.astype(jnp.bfloat16).reshape(master.shape[0], -1)
    long_kv = jnp.dot(long_acts, weights, preferred_element_type=jnp.float32)
    long_kv = long_kv.astype(jnp.bfloat16).reshape(long_acts.shape[0], master.shape[1], master.shape[2])
    return (new_master, new_first, new_second, long_kv)
```

```python
import jax
import jax.numpy as jnp
from jax import lax
from jax.experimental import pallas as pl
from jax.experimental.pallas import tpu as pltpu
from jax.sharding import PartitionSpec as P

beta_one = 0.9
beta_two = 0.95
learn_rate = 0.001
decay_rate = 0.1
adam_eps = 1e-08
steps_done = 100
fix_one = 1.0 - beta_one**steps_done
fix_two = 1.0 - beta_two**steps_done

F32, BF16 = jnp.float32, jnp.bfloat16
NZ = 8
NM = 8
ND = 32
FEAT = 1024
TOK = 1024
COL = 256
HALF = FEAT // 2
CH = HALF // NZ
ROWS = 256


def dp_index(xh, z, k):
    return xh * 16 + z * 2 + k


def mp_index(y, xl):
    return y * 2 + xl


def remote(src, dst, send_sem, recv_sem, dev):
    return pltpu.make_async_remote_copy(
        src_ref=src,
        dst_ref=dst,
        send_sem=send_sem,
        recv_sem=recv_sem,
        device_id=dev,
        device_id_type=pl.DeviceIdType.MESH,
    )


def kernel(
    acts_hbm, cot_hbm, mas_hbm, fir_hbm, sec_hbm, long_hbm,
    nm_ref, nf_ref, ns_ref, kv_ref,
    acts_v, acts_t, cots, prod, pair_out, pair_in, ring_out, ring_in, fin, land,
    state, fresh, arrived, w_all, long_v, acc,
    load_sem, cot_send, cot_recv, pair_send, pair_recv, ring_send, ring_recv,
    fin_send, land_recv, st_send, st_recv, x_sem, wr_send, wr_recv, sib_send, sib_recv,
):
    d, m = lax.axis_index("dp"), lax.axis_index("mp")
    xh, z, k = d // 16, (d // 2) % NZ, d % 2
    y, xl = m // 2, m % 2
    up, down = (z + 1) % NZ, (z + NZ - 1) % NZ
    yp, ym, yo = (y + 1) % 4, (y + 3) % 4, (y + 2) % 4
    xn = (d, mp_index(y, 1 - xl))
    dev_yp, dev_ym = (d, mp_index(yp, xl)), (d, mp_index(ym, xl))
    sib = (dp_index(xh, z, 1 - k), m)
    dev_up, dev_down = (dp_index(xh, up, k), m), (dp_index(xh, down, k), m)
    xpart = (dp_index(1 - xh, z, k), m)
    dt = dp_index(m // 4, 2 * (m % 4) + k, z // 4)
    src_m, src_k, src_z = d // 4, z % 2, k * 4

    loads = [
        pltpu.make_async_copy(cot_hbm, cots.at[m], load_sem.at[0]),
        pltpu.make_async_copy(acts_hbm, acts_v, load_sem.at[1]),
        pltpu.make_async_copy(mas_hbm, state.at[0], load_sem.at[2]),
        pltpu.make_async_copy(fir_hbm, state.at[1], load_sem.at[3]),
        pltpu.make_async_copy(sec_hbm, state.at[2], load_sem.at[4]),
        pltpu.make_async_copy(long_hbm, long_v, load_sem.at[5]),
    ]
    for load in loads:
        load.start()

    barrier = pltpu.get_barrier_semaphore()

    def greet(dev):
        pl.semaphore_signal(barrier, inc=1, device_id=dev, device_id_type=pl.DeviceIdType.MESH)

    for dev in (sib, dev_up, dev_down, xpart):
        greet(dev)
    for o in range(1, NM):
        greet((d, (m + o) % NM))
    for o in range(NM):
        greet((dt, (m + o) % NM))
    for a in range(2):
        for s in range(4):
            greet((dp_index(a, src_z + s, src_k), src_m))
    pl.semaphore_wait(barrier, 4 + NM - 1 + NM + 8)

    sends = []

    def go(copy):
        copy.start()
        sends.append(copy)
        return copy

    head = [
        m, mp_index(y, 1 - xl), mp_index(ym, xl), mp_index(yp, xl),
        mp_index(yo, xl), mp_index(ym, 1 - xl), mp_index(yp, 1 - xl), mp_index(yo, 1 - xl),
    ]
    low, high = pl.ds(0, TOK // 2), pl.ds(TOK // 2, TOK // 2)

    def cot_copy(n, block, dev):
        return remote(block, block, cot_send.at[n], cot_recv.at[n], dev)

    def cot_arrived(n, block):
        cot_copy(n, block, xn).wait_recv()

    def product(j):
        def tile(i, carry):
            rows = pl.multiple_of((1 - k) * HALF + i * 256, 256)
            pair_out[j, pl.ds(pl.multiple_of(i * 256, 256), 256), :] = jnp.dot(
                acts_t[pl.ds(rows, 256), :], cots[head[j]], preferred_element_type=F32
            ).astype(BF16)
            return carry

        lax.fori_loop(0, HALF // 256, tile, 0)
        go(remote(pair_out.at[j], pair_in.at[j], pair_send.at[j], pair_recv.at[j], sib))

        def mine(i, carry):
            rows = pl.multiple_of(k * HALF + i * 256, 256)
            prod[j, pl.ds(pl.multiple_of(i * 256, 256), 256), :] = jnp.dot(
                acts_t[pl.ds(rows, 256), :], cots[head[j]], preferred_element_type=F32
            )
            return carry

        lax.fori_loop(0, HALF // 256, mine, 0)

    def pair_arrived(j):
        remote(pair_out.at[j], pair_in.at[j], pair_send.at[j], pair_recv.at[j], sib).wait_recv()

    def ring_copy(g, r, s):
        return remote(
            ring_out.at[g, r, s], ring_in.at[g, r, s], ring_send.at[g, r, s], ring_recv.at[g, r, s],
            (dev_up, dev_down)[r],
        )

    def ring(g, s):
        for r in range(2):
            first = 4 * g + 2 * r
            chunk = (z + 2 * NZ - 1 - s) % NZ if r == 0 else (z + 1 + s) % NZ
            rows = pl.ds(pl.multiple_of(chunk * CH, CH), CH)
            total = prod[pl.ds(first, 2), rows, :] + pair_in[pl.ds(first, 2), rows, :].astype(F32)
            if s > 0:
                ring_copy(g, r, s - 1).wait_recv()
                total = total + ring_in[g, r, s - 1].astype(F32)
            if s < NZ - 1:
                ring_out[g, r, s] = total.astype(BF16)
                go(ring_copy(g, r, s))
            else:
                fin[pl.ds(first, 2)] = total.astype(BF16)
                for j in (first, first + 1):
                    hand_over(j)

    def final_copy(j):
        return remote(
            fin.at[j], land.at[xh, z % 4], fin_send.at[j], land_recv.at[xh, z % 4], (dt, head[j])
        )

    own_final = dt == d

    def hand_over(j):
        if j > 0:
            go(final_copy(j))
        else:

            @pl.when(own_final)
            def _():
                pltpu.make_async_copy(fin.at[0], land.at[xh, z % 4], land_recv.at[xh, z % 4]).start()

            @pl.when(jnp.logical_not(own_final))
            def _():
                final_copy(0).start()

    loads[0].wait()
    own = cots.at[m]
    go(cot_copy(0, own, xn))
    go(cot_copy(1, own, dev_yp))
    go(cot_copy(2, own, dev_ym))
    loads[1].wait()

    def turn(i, carry):
        rows = pl.ds(pl.multiple_of(i * 256, 256), 256)
        acts_t[rows, :] = acts_v[:, rows].T
        return carry

    lax.fori_loop(0, FEAT // 256, turn, 0)
    product(0)
    cot_arrived(1, cots.at[head[2]])
    go(cot_copy(3, cots.at[head[2], low], dev_yp))
    cot_arrived(2, cots.at[head[3]])
    go(cot_copy(4, cots.at[head[3], high], dev_ym))
    cot_arrived(0, cots.at[head[1]])
    go(cot_copy(5, cots.at[head[1]], dev_yp))
    go(cot_copy(6, cots.at[head[1]], dev_ym))
    for j in (1, 2, 3):
        product(j)
    for j in range(4):
        pair_arrived(j)
    ring(0, 0)
    cot_arrived(3, cots.at[head[4], low])
    go(cot_copy(7, cots.at[head[4], low], xn))
    cot_arrived(4, cots.at[head[4], high])
    go(cot_copy(8, cots.at[head[4], high], xn))
    product(4)
    ring(0, 1)
    ring(0, 2)
    cot_arrived(5, cots.at[head[5]])
    cot_arrived(6, cots.at[head[6]])
    product(5)
    product(6)
    ring(0, 3)
    cot_arrived(7, cots.at[head[7], low])
    cot_arrived(8, cots.at[head[7], high])
    product(7)
    for j in range(4, 8):
        pair_arrived(j)
    ring(1, 0)
    ring(0, 4)
    ring(1, 1)
    ring(0, 5)
    ring(1, 2)
    ring(0, 6)
    ring(1, 3)
    ring(0, 7)
    for s in range(4, NZ):
        ring(1, s)

    for n in (2, 3, 4):
        loads[n].wait()
    part = ROWS // 4
    for s in range(4):
        for a in range(2):
            remote(
                fin.at[0], land.at[a, s], fin_send.at[0], land_recv.at[a, s], xn
            ).wait_recv()
        rows = pl.ds(s * part, part)
        grad = land[0, s].astype(F32) + land[1, s].astype(F32)
        master, first, second = state[0, rows, :], state[1, rows, :], state[2, rows, :]
        first_next = beta_one * first + (1.0 - beta_one) * grad
        second_next = beta_two * second + (1.0 - beta_two) * grad * grad
        update = (
            first_next / fix_one / (jnp.sqrt(second_next / fix_two) + adam_eps)
            + decay_rate * master
        )
        master_next = master - learn_rate * update
        w_all[d, rows, :] = master_next.astype(BF16)
        for n, value in enumerate((master_next, first_next, second_next)):
            fresh[2 * s, n] = value[: part // 2]
            fresh[2 * s + 1, n] = value[part // 2 :]

    w_own = w_all.at[d]
    to_x = go(remote(w_own, w_own, x_sem.at[0], x_sem.at[1], xpart))
    top, bottom = pl.ds(0, ROWS // 2), pl.ds(ROWS // 2, ROWS // 2)

    def block_of(stream, r, s):
        at = (z + NZ - 1 - s) % NZ if r == 0 else (z + 1 + s) % NZ
        return dp_index(xh if stream == 0 else 1 - xh, at, k)

    def view(index, r, s):
        if s < 3:
            return w_all.at[index]
        return w_all.at[index, top if r == 0 else bottom]

    def weights_copy(stream, r, s):
        index = block_of(stream, r, s - 1) if s > 0 else dp_index(
            xh if stream == 0 else 1 - xh, z, k
        )
        src = view(index, r, s)
        return remote(
            src, src, wr_send.at[stream, r, s], wr_recv.at[stream, r, s], (dev_up, dev_down)[r]
        )

    def weights_arrived(stream, r, s):
        dst = view(block_of(stream, r, s), r, s)
        remote(
            dst, dst, wr_send.at[stream, r, s], wr_recv.at[stream, r, s], (dev_up, dev_down)[r]
        ).wait_recv()

    def to_sib(n, ref):
        go(remote(ref, ref, sib_send.at[n], sib_recv.at[n], sib))

    def sib_arrived(n, ref):
        remote(ref, ref, sib_send.at[n], sib_recv.at[n], sib).wait_recv()

    for r in range(2):
        go(weights_copy(0, r, 0))
    to_sib(0, w_own)

    def state_copy(o):
        to = (m + o) % NM
        return remote(fresh.at[to], arrived.at[m], st_send.at[o], st_recv.at[o], (d, to))

    for o in range(1, NM):
        go(state_copy(o))

    loads[5].wait()

    def add(index, start=False):
        cols = pl.ds(pl.multiple_of(index * ROWS, ROWS), ROWS)
        value = jnp.dot(long_v[:, cols], w_all[index], preferred_element_type=F32)
        if start:
            acc[...] = value
        else:
            acc[...] += value

    def other(index):
        return index + 1 - 2 * k

    add(d, True)
    sib_arrived(0, w_all.at[other(d)])
    add(other(d))
    across = dp_index(1 - xh, z, k)
    remote(w_all.at[across], w_all.at[across], x_sem.at[0], x_sem.at[1], xpart).wait_recv()
    for r in range(2):
        go(weights_copy(1, r, 0))
    to_sib(1, w_all.at[across])
    add(across)
    pending = [(1, w_all.at[other(across)], other(across))]
    for s in range(4):
        for stream in range(2):
            fresh_ones = []
            for r in range(2):
                weights_arrived(stream, r, s)
                if s < 3:
                    go(weights_copy(stream, r, s + 1))
                n = 2 + stream * 8 + s * 2 + r
                index = block_of(stream, r, s)
                to_sib(n, view(index, r, s))
                fresh_ones.append((n, index, r))
            for n, ref, index in pending:
                sib_arrived(n, ref)
                if index is not None:
                    add(index)
            pending = []
            for n, index, r in fresh_ones:
                whole = s < 3 or r == 1
                if whole:
                    add(index)
                pending.append((n, view(other(index), r, s), other(index) if whole else None))
        if s == 1:
            for n in range(3):
                arrived[m, n] = fresh[m, n]
            for o in range(1, NM):
                come = (m + NM - o) % NM
                remote(
                    fresh.at[m], arrived.at[come], st_send.at[o], st_recv.at[o], xn
                ).wait_recv()
            for h in range(NM):
                nm_ref[:, h, :] = arrived[h, 0]
                nf_ref[:, h, :] = arrived[h, 1]
                ns_ref[:, h, :] = arrived[h, 2]
    for n, ref, index in pending:
        sib_arrived(n, ref)
        if index is not None:
            add(index)
    kv_ref[...] = acc[...].astype(BF16)

    for copy in sends:
        copy.wait_send()

    @pl.when(jnp.logical_not(own_final))
    def _():
        final_copy(0).wait_send()


def on_device(acts, cotangent, master, first_moment, second_moment, long_acts):
    flat = [a.reshape(a.shape[0], -1) for a in (cotangent, master, first_moment, second_moment)]
    state_out = jax.ShapeDtypeStruct((ROWS // NM, NM, COL), F32)
    dma = pltpu.SemaphoreType.DMA
    outs = pl.pallas_call(
        kernel,
        out_shape=[state_out] * 3 + [jax.ShapeDtypeStruct((ROWS, COL), BF16)],
        in_specs=[pl.BlockSpec(memory_space=pl.ANY)] * 6,
        out_specs=[pl.BlockSpec(memory_space=pltpu.VMEM)] * 4,
        scratch_shapes=[
            pltpu.VMEM((TOK, FEAT), BF16),
            pltpu.VMEM((FEAT, TOK), BF16),
            pltpu.VMEM((NM, TOK, COL), BF16),
            pltpu.VMEM((NM, HALF, COL), F32),
            pltpu.VMEM((NM, HALF, COL), BF16),
            pltpu.VMEM((NM, HALF, COL), BF16),
            pltpu.VMEM((2, 2, NZ - 1, 2, CH, COL), BF16),
            pltpu.VMEM((2, 2, NZ - 1, 2, CH, COL), BF16),
            pltpu.VMEM((NM, CH, COL), BF16),
            pltpu.VMEM((2, 4, CH, COL), BF16),
            pltpu.VMEM((3, ROWS, COL), F32),
            pltpu.VMEM((NM, 3, ROWS // NM, COL), F32),
            pltpu.VMEM((NM, 3, ROWS // NM, COL), F32),
            pltpu.VMEM((ND, ROWS, COL), BF16),
            pltpu.VMEM((ROWS, ND * ROWS), BF16),
            pltpu.VMEM((ROWS, COL), F32),
            dma((6,)),
            dma((9,)),
            dma((9,)),
            dma((NM,)),
            dma((NM,)),
            dma((2, 2, NZ - 1)),
            dma((2, 2, NZ - 1)),
            dma((NM,)),
            dma((2, 4)),
            dma((NM,)),
            dma((NM,)),
            dma((2,)),
            dma((2, 2, 4)),
            dma((2, 2, 4)),
            dma((18,)),
            dma((18,)),
        ],
        compiler_params=pltpu.CompilerParams(
            collective_id=0, has_side_effects=True, vmem_limit_bytes=56 * 1024 * 1024
        ),
        cost_estimate=pl.CostEstimate(
            flops=2 * TOK * FEAT * NM * COL + 2 * ROWS * ND * ROWS * COL,
            bytes_accessed=8 * 1024 * 1024,
            transcendentals=0,
        ),
    )(acts, flat[0], flat[1], flat[2], flat[3], long_acts)
    return outs[0], outs[1], outs[2], outs[3].reshape(ROWS, 1, COL)


def solution(mesh):
    in_specs = (
        P("dp", "mp"),
        P("dp", "mp", None),
        P("dp", "mp", None),
        P("dp", "mp", None),
        P("dp", "mp", None),
        P("dp", None),
    )
    out_specs = (
        P(("dp", "mp"), None, None),
        P(("dp", "mp"), None, None),
        P(("dp", "mp"), None, None),
        P("dp", "mp", None),
    )
    return jax.shard_map(
        on_device, mesh=mesh, in_specs=in_specs, out_specs=out_specs, check_vma=False
    )
```

```python
import jax
import jax.numpy as jnp
from jax import lax
from jax.experimental import pallas as pl
from jax.experimental.pallas import tpu as pltpu
from jax.sharding import PartitionSpec as P

beta_one = 0.9
beta_two = 0.95
learn_rate = 0.001
decay_rate = 0.1
adam_eps = 1e-08
steps_done = 100
fix_one = 1.0 - beta_one**steps_done
fix_two = 1.0 - beta_two**steps_done

F32, BF16 = jnp.float32, jnp.bfloat16
NZ = 8
NM = 8
ND = 32
FEAT = 1024
TOK = 1024
COL = 256
HALF = FEAT // 2
CH = HALF // NZ
ROWS = 256


def dp_index(xh, z, k):
    return xh * 16 + z * 2 + k


def mp_index(y, xl):
    return y * 2 + xl


def remote(src, dst, send_sem, recv_sem, dev):
    return pltpu.make_async_remote_copy(
        src_ref=src,
        dst_ref=dst,
        send_sem=send_sem,
        recv_sem=recv_sem,
        device_id=dev,
        device_id_type=pl.DeviceIdType.MESH,
    )


def adamw(master, first, second, grad):
    first_next = beta_one * first + (1.0 - beta_one) * grad
    second_next = beta_two * second + (1.0 - beta_two) * grad * grad
    update = (
        first_next / fix_one / (jnp.sqrt(second_next / fix_two) + adam_eps) + decay_rate * master
    )
    return master - learn_rate * update, first_next, second_next


def kernel(
    acts_hbm, cot_hbm, mas_hbm, fir_hbm, sec_hbm, long_hbm,
    nm_hbm, nf_hbm, ns_hbm, kv_hbm,
    acts_v, acts_t, cots, prod, pair_out, pair_in, ring_out, ring_in, fin, land,
    raw, state, lent, grad_out, grad_in, fresh, arrived, out_v, w_all, long_v, acc, kv_v,
    load_sem, out_sem, cot_send, cot_recv, pair_send, pair_recv, ring_send, ring_recv,
    fin_send, land_recv, pre_send, pre_recv, post_send, post_recv,
    st_send, st_recv, x_sem, wr_send, wr_recv, sib_send, sib_recv,
):
    d, m = lax.axis_index("dp"), lax.axis_index("mp")
    xh, z, k = d // 16, (d // 2) % NZ, d % 2
    y, xl = m // 2, m % 2
    up, down = (z + 1) % NZ, (z + NZ - 1) % NZ
    yp, ym, yo = (y + 1) % 4, (y + 3) % 4, (y + 2) % 4
    xn = (d, mp_index(y, 1 - xl))
    dev_yp, dev_ym = (d, mp_index(yp, xl)), (d, mp_index(ym, xl))
    sib = (dp_index(xh, z, 1 - k), m)
    dev_up, dev_down = (dp_index(xh, up, k), m), (dp_index(xh, down, k), m)
    xpart = (dp_index(1 - xh, z, k), m)
    dt = dp_index(m // 4, z, k)

    def lender(zi, ki):
        return 4 * (z % 2) + 2 * k + zi, ki

    def owner(q):
        return 2 * q + z // 4, (z // 2) % 2

    loads = [
        pltpu.make_async_copy(cot_hbm, cots.at[m], load_sem.at[0]),
        pltpu.make_async_copy(acts_hbm, acts_v, load_sem.at[1]),
        pltpu.make_async_copy(mas_hbm, raw.at[0], load_sem.at[2]),
        pltpu.make_async_copy(fir_hbm, raw.at[1], load_sem.at[3]),
        pltpu.make_async_copy(sec_hbm, raw.at[2], load_sem.at[4]),
        pltpu.make_async_copy(long_hbm, long_v, load_sem.at[5]),
    ]
    for load in loads[:5]:
        load.start()

    barrier = pltpu.get_barrier_semaphore()

    def greet(dev):
        pl.semaphore_signal(barrier, inc=1, device_id=dev, device_id_type=pl.DeviceIdType.MESH)

    for dev in (sib, dev_up, dev_down, xpart):
        greet(dev)
    for o in range(1, NM):
        greet((d, (m + o) % NM))
    for o in range(NM):
        greet((dt, (m + o) % NM))
    for a in range(2):
        for q in range(4):
            greet((dp_index(a, z, k), 4 * xh + q))
    for zi in range(2):
        for ki in range(2):
            zt, kt = lender(zi, ki)
            greet((dp_index(xh, zt, kt), m))
    for q in range(4):
        zo, ko = owner(q)
        greet((dp_index(xh, zo, ko), m))
    pl.semaphore_wait(barrier, 4 + NM - 1 + NM + 8 + 4 + 4)

    sends = []

    def go(copy):
        copy.start()
        sends.append(copy)
        return copy

    def go_or_keep(here, src, dst, send_sem, recv_sem, dev):
        @pl.when(here)
        def _():
            pltpu.make_async_copy(src, dst, recv_sem).start()

        @pl.when(jnp.logical_not(here))
        def _():
            remote(src, dst, send_sem, recv_sem, dev).start()

    def sent_or_kept(here, src, dst, send_sem, recv_sem, dev):
        @pl.when(jnp.logical_not(here))
        def _():
            remote(src, dst, send_sem, recv_sem, dev).wait_send()

    head = [
        m, mp_index(y, 1 - xl), mp_index(ym, xl), mp_index(yp, xl),
        mp_index(yo, xl), mp_index(ym, 1 - xl), mp_index(yp, 1 - xl), mp_index(yo, 1 - xl),
    ]
    low, high = pl.ds(0, TOK // 2), pl.ds(TOK // 2, TOK // 2)

    def cot_copy(n, block, dev):
        return remote(block, block, cot_send.at[n], cot_recv.at[n], dev)

    def cot_arrived(n, block):
        cot_copy(n, block, xn).wait_recv()

    def product(j):
        def tile(i, carry):
            rows = pl.multiple_of((1 - k) * HALF + i * 256, 256)
            pair_out[j, pl.ds(pl.multiple_of(i * 256, 256), 256), :] = jnp.dot(
                acts_t[pl.ds(rows, 256), :], cots[head[j]], preferred_element_type=F32
            ).astype(BF16)
            return carry

        lax.fori_loop(0, HALF // 256, tile, 0)
        go(remote(pair_out.at[j], pair_in.at[j], pair_send.at[j], pair_recv.at[j], sib))

        def mine(i, carry):
            rows = pl.multiple_of(k * HALF + i * 256, 256)
            prod[j, pl.ds(pl.multiple_of(i * 256, 256), 256), :] = jnp.dot(
                acts_t[pl.ds(rows, 256), :], cots[head[j]], preferred_element_type=F32
            )
            return carry

        lax.fori_loop(0, HALF // 256, mine, 0)

    def pair_arrived(j):
        remote(pair_out.at[j], pair_in.at[j], pair_send.at[j], pair_recv.at[j], sib).wait_recv()

    def ring_copy(g, r, s):
        return remote(
            ring_out.at[g, r, s], ring_in.at[g, r, s], ring_send.at[g, r, s], ring_recv.at[g, r, s],
            (dev_up, dev_down)[r],
        )

    def ring(g, s):
        for r in range(2):
            j = 2 * g + r
            chunk = (z + 2 * NZ - 1 - s) % NZ if r == 0 else (z + 1 + s) % NZ
            rows = pl.ds(pl.multiple_of(chunk * CH, CH), CH)
            total = prod[j, rows, :] + pair_in[j, rows, :].astype(F32)
            if s > 0:
                ring_copy(g, r, s - 1).wait_recv()
                total = total + ring_in[g, r, s - 1].astype(F32)
            if s < NZ - 1:
                ring_out[g, r, s] = total.astype(BF16)
                go(ring_copy(g, r, s))
            else:
                fin[j] = total.astype(BF16)
                hand_over(j)

    def final_args(j):
        slot = (xh, m % 4)
        return (
            dt == d, fin.at[j], land.at[slot], fin_send.at[j], land_recv.at[slot], (dt, head[j])
        )

    def hand_over(j):
        if j > 0:
            go(remote(*final_args(j)[1:]))
        else:
            go_or_keep(*final_args(0))

    loads[0].wait()
    own = cots.at[m]
    go(cot_copy(0, own, xn))
    go(cot_copy(1, own, dev_yp))
    go(cot_copy(2, own, dev_ym))

    def lend_args(zi, ki):
        zt, kt = lender(zi, ki)
        rows = pl.ds(zi * 2 * CH + ki * CH, CH)
        return (
            (zt == z) & (kt == k), state.at[:, rows, :], lent.at[z // 2],
            pre_send.at[2 * zi + ki], pre_recv.at[z // 2], (dp_index(xh, zt, kt), m),
        )

    for n in range(3):
        loads[2 + n].wait()
        state[n] = raw[n, :, 0, :]
    for zi in range(2):
        for ki in range(2):
            go_or_keep(*lend_args(zi, ki))
    loads[5].start()
    loads[1].wait()

    def turn(i, carry):
        block = acts_v[:, pl.ds(pl.multiple_of(i * 2 * CH, 2 * CH), 2 * CH)].T
        at = pl.multiple_of(i * CH, CH)
        acts_t[pl.ds(at, CH), :] = block[:CH]
        acts_t[pl.ds(at + HALF, CH), :] = block[CH:]
        return carry

    lax.fori_loop(0, NZ, turn, 0)
    product(0)
    cot_arrived(1, cots.at[head[2]])
    go(cot_copy(3, cots.at[head[2], low], dev_yp))
    cot_arrived(2, cots.at[head[3]])
    go(cot_copy(4, cots.at[head[3], high], dev_ym))
    cot_arrived(0, cots.at[head[1]])
    go(cot_copy(5, cots.at[head[1]], dev_yp))
    go(cot_copy(6, cots.at[head[1]], dev_ym))
    product(1)
    product(2)
    product(3)
    for j in range(2):
        pair_arrived(j)
    ring(0, 0)
    for j in range(2, 4):
        pair_arrived(j)
    ring(1, 0)
    cot_arrived(3, cots.at[head[4], low])
    go(cot_copy(7, cots.at[head[4], low], xn))
    cot_arrived(4, cots.at[head[4], high])
    go(cot_copy(8, cots.at[head[4], high], xn))
    product(4)
    for s in range(1, NZ - 1):
        ring(0, s)
        ring(1, s)
    cot_arrived(5, cots.at[head[5]])
    product(5)
    cot_arrived(6, cots.at[head[6]])
    product(6)
    pair_arrived(4)
    pair_arrived(5)
    ring(2, 0)
    cot_arrived(7, cots.at[head[7], low])
    cot_arrived(8, cots.at[head[7], high])
    product(7)
    pair_arrived(6)
    pair_arrived(7)
    ring(3, 0)
    ring(0, NZ - 1)
    ring(1, NZ - 1)
    for s in range(1, NZ):
        ring(2, s)
        ring(3, s)

    place = xh * NZ + z
    half_rows = pl.ds(pl.multiple_of(k * CH, CH), CH)
    for q in range(4):
        remote(
            state.at[:, pl.ds(0, CH), :], lent.at[q], pre_send.at[0], pre_recv.at[q], xn
        ).wait_recv()
    for q in range(4):
        for a in range(2):
            remote(
                fin.at[0], land.at[a, q], fin_send.at[0], land_recv.at[a, q], xn
            ).wait_recv()
        grad = (land[0, q].astype(F32) + land[1, q].astype(F32)).astype(BF16)
        grad_out[q] = grad
        w_all[place, q, half_rows, :] = adamw(
            lent[q, 0], lent[q, 1], lent[q, 2], grad.astype(F32)
        )[0].astype(BF16)

    other_rows = pl.ds(pl.multiple_of((1 - k) * CH, CH), CH)

    def view(at, r=0, s=0, rows=half_rows):
        if s < 3:
            return w_all.at[at, :, rows, :]
        return w_all.at[at, pl.ds(2 * r, 2), rows, :]

    w_own = view(place)
    go(remote(w_own, w_own, x_sem.at[0], x_sem.at[1], xpart))

    def block_of(stream, r, s):
        at = (z + NZ - 1 - s) % NZ if r == 0 else (z + 1 + s) % NZ
        return (xh if stream == 0 else 1 - xh) * NZ + at

    def weights_copy(stream, r, s):
        src = view(block_of(stream, r, s - 1), r, s)
        return remote(
            src, src, wr_send.at[stream, r, s], wr_recv.at[stream, r, s], (dev_up, dev_down)[r]
        )

    def weights_arrived(stream, r, s):
        dst = view(block_of(stream, r, s), r, s)
        remote(
            dst, dst, wr_send.at[stream, r, s], wr_recv.at[stream, r, s], (dev_up, dev_down)[r]
        ).wait_recv()

    def to_sib(n, ref):
        go(remote(ref, ref, sib_send.at[n], sib_recv.at[n], sib))

    def sib_arrived(n, ref):
        remote(ref, ref, sib_send.at[n], sib_recv.at[n], sib).wait_recv()

    for r in range(2):
        go(weights_copy(0, r, 0))
    to_sib(0, w_own)

    def post_args(q):
        zo, ko = owner(q)
        slot = 2 * (z % 2) + k
        return (
            (zo == z) & (ko == k), grad_out.at[q], grad_in.at[slot],
            post_send.at[q], post_recv.at[slot], (dp_index(xh, zo, ko), m),
        )

    for q in range(4):
        go_or_keep(*post_args(q))

    loads[5].wait()

    def add(at, start=False):
        value = 0.0
        for q in range(4):
            cols = ((at // NZ) * 4 + q) * FEAT + (at % NZ) * 2 * CH
            value += jnp.dot(
                long_v[:, pl.ds(pl.multiple_of(cols, 2 * CH), 2 * CH)],
                w_all[at, q],
                preferred_element_type=F32,
            )
        if start:
            acc[...] = value
        else:
            acc[...] += value

    across = (1 - xh) * NZ + z
    w_across = view(across)
    remote(w_across, w_across, x_sem.at[0], x_sem.at[1], xpart).wait_recv()
    for r in range(2):
        go(weights_copy(1, r, 0))
    to_sib(1, w_across)
    sib_arrived(0, view(place, rows=other_rows))
    add(place, True)

    def state_copy(o):
        to = (m + o) % NM
        return remote(fresh.at[to], arrived.at[m], st_send.at[o], st_recv.at[o], (d, to))

    outs = [
        pltpu.make_async_copy(out_v.at[n], ref, out_sem.at[n])
        for n, ref in enumerate((nm_hbm, nf_hbm, ns_hbm))
    ]
    pending = [(1, view(across, rows=other_rows), across)]
    for s in range(4):
        for stream in range(2):
            come = []
            for r in range(2):
                weights_arrived(stream, r, s)
                if s < 3:
                    go(weights_copy(stream, r, s + 1))
                n = 2 + stream * 8 + s * 2 + r
                at = block_of(stream, r, s)
                to_sib(n, view(at, r, s))
                whole = s < 3 or r == 1
                come.append((n, view(at, r, s, other_rows), at if whole else None))
            for n, ref, at in pending:
                sib_arrived(n, ref)
                if at is not None:
                    add(at)
            pending = come
        if s == 0:
            for n in range(4):
                remote(
                    grad_out.at[0], grad_in.at[n], post_send.at[0], post_recv.at[n], xn
                ).wait_recv()
                rows = pl.ds(n * CH, CH)
                new = adamw(
                    state[0, rows, :], state[1, rows, :], state[2, rows, :], grad_in[n].astype(F32)
                )
                for a, value in enumerate(new):
                    fresh[2 * n, a] = value[: CH // 2]
                    fresh[2 * n + 1, a] = value[CH // 2 :]
            for o in range(1, NM):
                go(state_copy(o))
        if s == 2:
            for a in range(3):
                arrived[m, a] = fresh[m, a]
            for o in range(1, NM):
                at = (m + NM - o) % NM
                remote(fresh.at[m], arrived.at[at], st_send.at[o], st_recv.at[o], xn).wait_recv()
            for a in range(3):
                for h in range(NM):
                    out_v[a, :, h, :] = arrived[h, a]
                outs[a].start()
    for n, ref, at in pending:
        sib_arrived(n, ref)
        if at is not None:
            add(at)
    kv_v[...] = acc[...].astype(BF16)
    kv_out = pltpu.make_async_copy(kv_v, kv_hbm, out_sem.at[3])
    kv_out.start()

    for copy in sends:
        copy.wait_send()
    sent_or_kept(*final_args(0))
    for n in range(4):
        sent_or_kept(*lend_args(n // 2, n % 2))
        sent_or_kept(*post_args(n))
    for out in outs:
        out.wait()
    kv_out.wait()


def settle(a_hbm, b_hbm, c_hbm, e_hbm, ao_hbm, bo_hbm, co_hbm, eo_hbm, sem):
    pairs = ((a_hbm, ao_hbm), (b_hbm, bo_hbm), (c_hbm, co_hbm), (e_hbm, eo_hbm))
    copies = [pltpu.make_async_copy(a, b, sem.at[n]) for n, (a, b) in enumerate(pairs)]
    for copy in copies:
        copy.start()
    for copy in copies:
        copy.wait()


def on_device(acts, cotangent, master, first_moment, second_moment, long_acts):
    state_out = jax.ShapeDtypeStruct((ROWS // NM, NM, COL), F32)
    out_shape = [state_out] * 3 + [jax.ShapeDtypeStruct((ROWS, COL), BF16)]
    dma = pltpu.SemaphoreType.DMA
    anywhere = pl.BlockSpec(memory_space=pl.ANY)
    outs = pl.pallas_call(
        kernel,
        out_shape=out_shape,
        in_specs=[anywhere] * 6,
        out_specs=[anywhere] * 4,
        scratch_shapes=[
            pltpu.VMEM((TOK, FEAT), BF16),
            pltpu.VMEM((FEAT, TOK), BF16),
            pltpu.VMEM((NM, TOK, COL), BF16),
            pltpu.VMEM((NM, HALF, COL), F32),
            pltpu.VMEM((NM, HALF, COL), BF16),
            pltpu.VMEM((NM, HALF, COL), BF16),
            pltpu.VMEM((4, 2, NZ - 1, CH, COL), BF16),
            pltpu.VMEM((4, 2, NZ - 1, CH, COL), BF16),
            pltpu.VMEM((NM, CH, COL), BF16),
            pltpu.VMEM((2, 4, CH, COL), BF16),
            pltpu.VMEM((3, ROWS, 1, COL), F32),
            pltpu.VMEM((3, ROWS, COL), F32),
            pltpu.VMEM((4, 3, CH, COL), F32),
            pltpu.VMEM((4, CH, COL), BF16),
            pltpu.VMEM((4, CH, COL), BF16),
            pltpu.VMEM((NM, 3, ROWS // NM, COL), F32),
            pltpu.VMEM((NM, 3, ROWS // NM, COL), F32),
            pltpu.VMEM((3, ROWS // NM, NM, COL), F32),
            pltpu.VMEM((ND // 2, 4, 2 * CH, COL), BF16),
            pltpu.VMEM((ROWS, ND * ROWS), BF16),
            pltpu.VMEM((ROWS, COL), F32),
            pltpu.VMEM((ROWS, COL), BF16),
            dma((6,)),
            dma((4,)),
            dma((9,)),
            dma((9,)),
            dma((NM,)),
            dma((NM,)),
            dma((4, 2, NZ - 1)),
            dma((4, 2, NZ - 1)),
            dma((NM,)),
            dma((2, 4)),
            dma((4,)),
            dma((4,)),
            dma((4,)),
            dma((4,)),
            dma((NM,)),
            dma((NM,)),
            dma((2,)),
            dma((2, 2, 4)),
            dma((2, 2, 4)),
            dma((18,)),
            dma((18,)),
        ],
        compiler_params=pltpu.CompilerParams(
            collective_id=0, has_side_effects=True, vmem_limit_bytes=56 * 1024 * 1024
        ),
        cost_estimate=pl.CostEstimate(
            flops=2 * TOK * FEAT * NM * COL + 2 * ROWS * ND * ROWS * COL,
            bytes_accessed=8 * 1024 * 1024,
            transcendentals=0,
        ),
    )(acts, cotangent.reshape(TOK, COL), master, first_moment, second_moment, long_acts)
    outs = pl.pallas_call(
        settle,
        out_shape=out_shape,
        in_specs=[anywhere] * 4,
        out_specs=[anywhere] * 4,
        scratch_shapes=[dma((4,))],
    )(*outs)
    return outs[0], outs[1], outs[2], outs[3].reshape(ROWS, 1, COL)


def solution(mesh):
    in_specs = (
        P("dp", "mp"),
        P("dp", "mp", None),
        P("dp", "mp", None),
        P("dp", "mp", None),
        P("dp", "mp", None),
        P("dp", None),
    )
    out_specs = (
        P(("dp", "mp"), None, None),
        P(("dp", "mp"), None, None),
        P(("dp", "mp"), None, None),
        P("dp", "mp", None),
    )
    return jax.shard_map(
        on_device, mesh=mesh, in_specs=in_specs, out_specs=out_specs, check_vma=False
    )
```

```python
import jax
import jax.numpy as jnp
from jax import lax
from jax.experimental import pallas as pl
from jax.experimental.pallas import tpu as pltpu
from jax.sharding import PartitionSpec as P

beta_one = 0.9
beta_two = 0.95
learn_rate = 0.001
decay_rate = 0.1
adam_eps = 1e-08
steps_done = 100
fix_one = 1.0 - beta_one**steps_done
fix_two = 1.0 - beta_two**steps_done

F32, BF16 = jnp.float32, jnp.bfloat16
NZ = 8
NM = 8
ND = 32
FEAT = 1024
TOK = 1024
COL = 256
HALF = FEAT // 2
CH = HALF // NZ
ROWS = 256


def dp_index(xh, z, k):
    return xh * 16 + z * 2 + k


def mp_index(y, xl):
    return y * 2 + xl


def remote(src, dst, send_sem, recv_sem, dev):
    return pltpu.make_async_remote_copy(
        src_ref=src,
        dst_ref=dst,
        send_sem=send_sem,
        recv_sem=recv_sem,
        device_id=dev,
        device_id_type=pl.DeviceIdType.MESH,
    )


def adamw(master, first, second, grad):
    first_next = beta_one * first + (1.0 - beta_one) * grad
    second_next = beta_two * second + (1.0 - beta_two) * grad * grad
    update = (
        first_next / fix_one / (jnp.sqrt(second_next / fix_two) + adam_eps) + decay_rate * master
    )
    return master - learn_rate * update, first_next, second_next


def kernel(
    acts_hbm, cot_hbm, mas_hbm, fir_hbm, sec_hbm, long_hbm,
    nm_hbm, nf_hbm, ns_hbm, kv_hbm,
    acts_v, acts_t, cots, prod, pair_out, pair_in, ring_out, ring_in, fin, land,
    raw, state, lent, grad_out, grad_in, fresh, arrived, out_v, w_all, long_v, acc, kv_v,
    load_sem, out_sem, cot_send, cot_recv, pair_send, pair_recv, ring_send, ring_recv,
    fin_send, land_recv, pre_send, pre_recv, post_send, post_recv,
    st_send, st_recv, x_send, x_recv, wr_send, wr_recv, sib_send, sib_recv,
):
    d, m = lax.axis_index("dp"), lax.axis_index("mp")
    xh, z, k = d // 16, (d // 2) % NZ, d % 2
    y, xl = m // 2, m % 2
    up, down = (z + 1) % NZ, (z + NZ - 1) % NZ
    yp, ym, yo = (y + 1) % 4, (y + 3) % 4, (y + 2) % 4
    xn = (d, mp_index(y, 1 - xl))
    dev_yp, dev_ym = (d, mp_index(yp, xl)), (d, mp_index(ym, xl))
    sib = (dp_index(xh, z, 1 - k), m)
    dev_up, dev_down = (dp_index(xh, up, k), m), (dp_index(xh, down, k), m)
    xpart = (dp_index(1 - xh, z, k), m)
    dt = dp_index(m // 4, z, k)

    def lender(zi, ki):
        return 4 * (z % 2) + 2 * k + zi, ki

    def owner(q):
        return 2 * q + z // 4, (z // 2) % 2

    loads = [
        pltpu.make_async_copy(cot_hbm, cots.at[m], load_sem.at[0]),
        pltpu.make_async_copy(acts_hbm, acts_v, load_sem.at[1]),
        pltpu.make_async_copy(mas_hbm, raw.at[0], load_sem.at[2]),
        pltpu.make_async_copy(fir_hbm, raw.at[1], load_sem.at[3]),
        pltpu.make_async_copy(sec_hbm, raw.at[2], load_sem.at[4]),
        pltpu.make_async_copy(long_hbm, long_v, load_sem.at[5]),
    ]
    for load in loads[:5]:
        load.start()

    barrier = pltpu.get_barrier_semaphore()

    def greet(dev):
        pl.semaphore_signal(barrier, inc=1, device_id=dev, device_id_type=pl.DeviceIdType.MESH)

    for dev in (sib, dev_up, dev_down, xpart):
        greet(dev)
    for o in range(1, NM):
        greet((d, (m + o) % NM))
    for o in range(NM):
        greet((dt, (m + o) % NM))
    for a in range(2):
        for q in range(4):
            greet((dp_index(a, z, k), 4 * xh + q))
    for zi in range(2):
        for ki in range(2):
            zt, kt = lender(zi, ki)
            greet((dp_index(xh, zt, kt), m))
    for q in range(4):
        zo, ko = owner(q)
        greet((dp_index(xh, zo, ko), m))
    pl.semaphore_wait(barrier, 4 + NM - 1 + NM + 8 + 4 + 4)

    sends = []

    def go(copy):
        copy.start()
        sends.append(copy)
        return copy

    def go_or_keep(here, src, dst, send_sem, recv_sem, dev):
        @pl.when(here)
        def _():
            pltpu.make_async_copy(src, dst, recv_sem).start()

        @pl.when(jnp.logical_not(here))
        def _():
            remote(src, dst, send_sem, recv_sem, dev).start()

    def sent_or_kept(here, src, dst, send_sem, recv_sem, dev):
        @pl.when(jnp.logical_not(here))
        def _():
            remote(src, dst, send_sem, recv_sem, dev).wait_send()

    head = [
        m, mp_index(y, 1 - xl), mp_index(ym, xl), mp_index(yp, xl),
        mp_index(yo, xl), mp_index(ym, 1 - xl), mp_index(yp, 1 - xl), mp_index(yo, 1 - xl),
    ]
    low, high = pl.ds(0, TOK // 2), pl.ds(TOK // 2, TOK // 2)

    def cot_copy(n, block, dev):
        return remote(block, block, cot_send.at[n], cot_recv.at[n], dev)

    def cot_arrived(n, block):
        cot_copy(n, block, xn).wait_recv()

    def product(j):
        def tile(i, carry):
            rows = pl.multiple_of((1 - k) * HALF + i * 256, 256)
            pair_out[j, pl.ds(pl.multiple_of(i * 256, 256), 256), :] = jnp.dot(
                acts_t[pl.ds(rows, 256), :], cots[head[j]], preferred_element_type=F32
            ).astype(BF16)
            return carry

        lax.fori_loop(0, HALF // 256, tile, 0)
        go(remote(pair_out.at[j], pair_in.at[j], pair_send.at[j], pair_recv.at[j], sib))

        def mine(i, carry):
            rows = pl.multiple_of(k * HALF + i * 256, 256)
            prod[j, pl.ds(pl.multiple_of(i * 256, 256), 256), :] = jnp.dot(
                acts_t[pl.ds(rows, 256), :], cots[head[j]], preferred_element_type=F32
            )
            return carry

        lax.fori_loop(0, HALF // 256, mine, 0)

    def pair_arrived(j):
        remote(pair_out.at[j], pair_in.at[j], pair_send.at[j], pair_recv.at[j], sib).wait_recv()

    def part(s, r):
        return pl.ds(r * CH // 2, CH // 2) if s == 0 else pl.ds(0, CH)

    def ring_copy(j, r, s):
        return remote(
            ring_out.at[j, r, s, part(s, r)], ring_in.at[j, r, s, part(s, r)],
            ring_send.at[j, r, s], ring_recv.at[j, r, s], (dev_up, dev_down)[r],
        )

    def own_part(j, chunk, first, size):
        rows = pl.ds(pl.multiple_of(chunk * CH + first, CH // 2), size)
        return prod[j, rows, :] + pair_in[j, rows, :].astype(F32)

    def ring(j, s):
        for r in range(2):
            chunk = (z + NZ // 2 - s) % NZ if r == 0 else (z + NZ // 2 + s) % NZ
            if s == 0:
                ring_out[j, r, s, part(s, r)] = own_part(
                    j, chunk, r * CH // 2, CH // 2
                ).astype(BF16)
            elif s == 1:
                mine, theirs = part(0, r), part(0, 1 - r)
                ring_out[j, r, s, theirs] = own_part(
                    j, chunk, (1 - r) * CH // 2, CH // 2
                ).astype(BF16)
                total = own_part(j, chunk, r * CH // 2, CH // 2)
                ring_copy(j, r, 0).wait_recv()
                ring_out[j, r, s, mine] = (total + ring_in[j, r, 0, mine].astype(F32)).astype(BF16)
            else:
                total = own_part(j, chunk, 0, CH)
                ring_copy(j, r, s - 1).wait_recv()
                ring_out[j, r, s] = (total + ring_in[j, r, s - 1].astype(F32)).astype(BF16)
            go(ring_copy(j, r, s))

    def finish(j):
        total = own_part(j, z, 0, CH)
        for r in range(2):
            ring_copy(j, r, 3).wait_recv()
            total = total + ring_in[j, r, 3].astype(F32)
        fin[j] = total.astype(BF16)
        hand_over(j)

    def final_args(j):
        slot = (xh, m % 4)
        return (
            dt == d, fin.at[j], land.at[slot], fin_send.at[j], land_recv.at[slot], (dt, head[j])
        )

    def hand_over(j):
        if j > 0:
            go(remote(*final_args(j)[1:]))
        else:
            go_or_keep(*final_args(0))

    loads[0].wait()
    def half(j, side):
        return cots.at[head[j], (low, high)[side]]

    go(cot_copy(0, half(0, 0), xn))
    go(cot_copy(2, half(0, 0), dev_yp))
    go(cot_copy(4, half(0, 1), dev_ym))
    go(cot_copy(1, half(0, 1), xn))
    go(cot_copy(3, half(0, 1), dev_yp))
    go(cot_copy(5, half(0, 0), dev_ym))

    def lend_args(zi, ki):
        zt, kt = lender(zi, ki)
        rows = pl.ds(zi * 2 * CH + ki * CH, CH)
        return (
            (zt == z) & (kt == k), state.at[:, rows, :], lent.at[z // 2],
            pre_send.at[2 * zi + ki], pre_recv.at[z // 2], (dp_index(xh, zt, kt), m),
        )

    for n in range(3):
        loads[2 + n].wait()
        state[n] = raw[n, :, 0, :]
    for zi in range(2):
        for ki in range(2):
            go_or_keep(*lend_args(zi, ki))
    loads[5].start()
    loads[1].wait()

    def turn(i, carry):
        block = acts_v[:, pl.ds(pl.multiple_of(i * 2 * CH, 2 * CH), 2 * CH)].T
        at = pl.multiple_of(i * CH, CH)
        acts_t[pl.ds(at, CH), :] = block[:CH]
        acts_t[pl.ds(at + HALF, CH), :] = block[CH:]
        return carry

    lax.fori_loop(0, NZ, turn, 0)
    product(0)
    cot_arrived(2, half(2, 0))
    go(cot_copy(6, half(2, 0), dev_yp))
    cot_arrived(4, half(3, 1))
    go(cot_copy(7, half(3, 1), dev_ym))
    for side in range(2):
        cot_arrived(side, half(1, side))
        go(cot_copy(8 + side, half(1, side), dev_yp))
        go(cot_copy(10 + side, half(1, side), dev_ym))
    product(1)
    cot_arrived(3, half(2, 1))
    product(2)
    cot_arrived(5, half(3, 0))
    product(3)
    for j in range(4):
        pair_arrived(j)
        ring(j, 0)
    cot_arrived(6, half(4, 0))
    go(cot_copy(12, half(4, 0), xn))
    cot_arrived(7, half(4, 1))
    go(cot_copy(13, half(4, 1), xn))
    product(4)
    for j in range(4):
        ring(j, 1)
    pair_arrived(4)
    ring(4, 0)
    for s in range(2, 4):
        for j in range(4):
            ring(j, s)
        ring(4, s - 1)
    for j in range(5, 8):
        for side in range(2):
            cot_arrived(2 * j - 2 + side, half(j, side))
        product(j)
    for j in range(5, 8):
        pair_arrived(j)
        ring(j, 0)
    ring(4, 3)
    for j in range(4):
        finish(j)
    for j in range(5, 8):
        ring(j, 1)
    finish(4)
    for s in range(2, 4):
        for j in range(5, 8):
            ring(j, s)
    for j in range(5, 8):
        finish(j)

    place = xh * NZ + z
    half_rows = pl.ds(pl.multiple_of(k * CH, CH), CH)
    for q in range(4):
        remote(
            state.at[:, pl.ds(0, CH), :], lent.at[q], pre_send.at[0], pre_recv.at[q], xn
        ).wait_recv()
    for q in range(4):
        for a in range(2):
            remote(
                fin.at[0], land.at[a, q], fin_send.at[0], land_recv.at[a, q], xn
            ).wait_recv()
        grad = (land[0, q].astype(F32) + land[1, q].astype(F32)).astype(BF16)
        grad_out[q] = grad
        w_all[place, q, half_rows, :] = adamw(
            lent[q, 0], lent[q, 1], lent[q, 2], grad.astype(F32)
        )[0].astype(BF16)

    other_rows = pl.ds(pl.multiple_of((1 - k) * CH, CH), CH)

    def view(at, p, rows=half_rows):
        return w_all.at[at, pl.ds(2 * p, 2), rows, :]

    def x_copy(at, p):
        return remote(view(at, p), view(at, p), x_send.at[p], x_recv.at[p], xpart)

    def block_of(stream, r, s):
        at = (z + NZ - 1 - s) % NZ if r == 0 else (z + 1 + s) % NZ
        return (xh if stream == 0 else 1 - xh) * NZ + at

    def halves(r, s):
        return range(2) if s < 3 else (r,)

    def weights_copy(stream, r, s, p):
        src = view(block_of(stream, r, s - 1), p)
        return remote(
            src, src, wr_send.at[stream, r, s, p], wr_recv.at[stream, r, s, p],
            (dev_up, dev_down)[r],
        )

    def weights_arrived(stream, r, s, p):
        dst = view(block_of(stream, r, s), p)
        remote(
            dst, dst, wr_send.at[stream, r, s, p], wr_recv.at[stream, r, s, p],
            (dev_up, dev_down)[r],
        ).wait_recv()

    def to_sib(n, ref):
        go(remote(ref, ref, sib_send.at[n], sib_recv.at[n], sib))

    def sib_arrived(n, ref):
        remote(ref, ref, sib_send.at[n], sib_recv.at[n], sib).wait_recv()

    for p in range(2):
        go(x_copy(place, p))
        for r in range(2):
            go(weights_copy(0, r, 0, p))
    for p in range(2):
        to_sib(p, view(place, p))

    def post_args(q):
        zo, ko = owner(q)
        slot = 2 * (z % 2) + k
        return (
            (zo == z) & (ko == k), grad_out.at[q], grad_in.at[slot],
            post_send.at[q], post_recv.at[slot], (dp_index(xh, zo, ko), m),
        )

    for q in range(4):
        go_or_keep(*post_args(q))

    loads[5].wait()

    def add(at, start=False):
        value = 0.0
        for q in range(4):
            cols = ((at // NZ) * 4 + q) * FEAT + (at % NZ) * 2 * CH
            value += jnp.dot(
                long_v[:, pl.ds(pl.multiple_of(cols, 2 * CH), 2 * CH)],
                w_all[at, q],
                preferred_element_type=F32,
            )
        if start:
            acc[...] = value
        else:
            acc[...] += value

    across = (1 - xh) * NZ + z
    for p in range(2):
        x_copy(across, p).wait_recv()
        for r in range(2):
            go(weights_copy(1, r, 0, p))
        to_sib(2 + p, view(across, p))
    for p in range(2):
        sib_arrived(p, view(place, p, other_rows))
    add(place, True)

    def state_copy(o):
        to = (m + o) % NM
        return remote(fresh.at[to], arrived.at[m], st_send.at[o], st_recv.at[o], (d, to))

    outs = [
        pltpu.make_async_copy(out_v.at[n], ref, out_sem.at[n])
        for n, ref in enumerate((nm_hbm, nf_hbm, ns_hbm))
    ]
    pending = [(2, across, 0, False), (3, across, 1, True)]

    def catch_up():
        for n, at, p, last in pending:
            sib_arrived(n, view(at, p, other_rows))
            if last:
                add(at)

    for s in range(4):
        for stream in range(2):
            come = []
            for r in range(2):
                for p in halves(r, s):
                    weights_arrived(stream, r, s, p)
                    if s < 2 or (s == 2 and p == r):
                        go(weights_copy(stream, r, s + 1, p))
                    n = 4 + stream * 16 + s * 4 + r * 2 + p
                    at = block_of(stream, r, s)
                    to_sib(n, view(at, p))
                    come.append((n, at, p, p == 1))
            catch_up()
            pending = come
        if s == 0:
            for n in range(4):
                remote(
                    grad_out.at[0], grad_in.at[n], post_send.at[0], post_recv.at[n], xn
                ).wait_recv()
                rows = pl.ds(n * CH, CH)
                new = adamw(
                    state[0, rows, :], state[1, rows, :], state[2, rows, :], grad_in[n].astype(F32)
                )
                for a, value in enumerate(new):
                    fresh[2 * n, a] = value[: CH // 2]
                    fresh[2 * n + 1, a] = value[CH // 2 :]
            for o in range(1, NM):
                go(state_copy(o))
        if s == 2:
            for a in range(3):
                arrived[m, a] = fresh[m, a]
            for o in range(1, NM):
                at = (m + NM - o) % NM
                remote(fresh.at[m], arrived.at[at], st_send.at[o], st_recv.at[o], xn).wait_recv()
            for a in range(3):
                for h in range(NM):
                    out_v[a, :, h, :] = arrived[h, a]
                outs[a].start()
    catch_up()
    kv_v[...] = acc[...].astype(BF16)
    kv_out = pltpu.make_async_copy(kv_v, kv_hbm, out_sem.at[3])
    kv_out.start()

    for copy in sends:
        copy.wait_send()
    sent_or_kept(*final_args(0))
    for n in range(4):
        sent_or_kept(*lend_args(n // 2, n % 2))
        sent_or_kept(*post_args(n))
    for out in outs:
        out.wait()
    kv_out.wait()


def settle(a_ref, b_ref, c_ref, e_ref, a_hbm, b_hbm, c_hbm, e_hbm, sem):
    pairs = ((a_ref, a_hbm), (b_ref, b_hbm), (c_ref, c_hbm), (e_ref, e_hbm))
    copies = [pltpu.make_async_copy(a, b, sem.at[n]) for n, (a, b) in enumerate(pairs)]
    for copy in copies:
        copy.start()
    for copy in copies:
        copy.wait()


def on_device(acts, cotangent, master, first_moment, second_moment, long_acts):
    state_out = jax.ShapeDtypeStruct((ROWS // NM, NM, COL), F32)
    out_shape = [state_out] * 3 + [jax.ShapeDtypeStruct((ROWS, COL), BF16)]
    dma = pltpu.SemaphoreType.DMA
    anywhere = pl.BlockSpec(memory_space=pl.ANY)
    outs = pl.pallas_call(
        kernel,
        out_shape=out_shape,
        in_specs=[anywhere] * 6,
        out_specs=[anywhere] * 4,
        scratch_shapes=[
            pltpu.VMEM((TOK, FEAT), BF16),
            pltpu.VMEM((FEAT, TOK), BF16),
            pltpu.VMEM((NM, TOK, COL), BF16),
            pltpu.VMEM((NM, HALF, COL), F32),
            pltpu.VMEM((NM, HALF, COL), BF16),
            pltpu.VMEM((NM, HALF, COL), BF16),
            pltpu.VMEM((NM, 2, 4, CH, COL), BF16),
            pltpu.VMEM((NM, 2, 4, CH, COL), BF16),
            pltpu.VMEM((NM, CH, COL), BF16),
            pltpu.VMEM((2, 4, CH, COL), BF16),
            pltpu.VMEM((3, ROWS, 1, COL), F32),
            pltpu.VMEM((3, ROWS, COL), F32),
            pltpu.VMEM((4, 3, CH, COL), F32),
            pltpu.VMEM((4, CH, COL), BF16),
            pltpu.VMEM((4, CH, COL), BF16),
            pltpu.VMEM((NM, 3, ROWS // NM, COL), F32),
            pltpu.VMEM((NM, 3, ROWS // NM, COL), F32),
            pltpu.VMEM((3, ROWS // NM, NM, COL), F32),
            pltpu.VMEM((ND // 2, 4, 2 * CH, COL), BF16),
            pltpu.VMEM((ROWS, ND * ROWS), BF16),
            pltpu.VMEM((ROWS, COL), F32),
            pltpu.VMEM((ROWS, COL), BF16),
            dma((6,)),
            dma((4,)),
            dma((14,)),
            dma((14,)),
            dma((NM,)),
            dma((NM,)),
            dma((NM, 2, 4)),
            dma((NM, 2, 4)),
            dma((NM,)),
            dma((2, 4)),
            dma((4,)),
            dma((4,)),
            dma((4,)),
            dma((4,)),
            dma((NM,)),
            dma((NM,)),
            dma((2,)),
            dma((2,)),
            dma((2, 2, 4, 2)),
            dma((2, 2, 4, 2)),
            dma((36,)),
            dma((36,)),
        ],
        compiler_params=pltpu.CompilerParams(
            collective_id=0, has_side_effects=True, vmem_limit_bytes=56 * 1024 * 1024
        ),
        cost_estimate=pl.CostEstimate(
            flops=2 * TOK * FEAT * NM * COL + 2 * ROWS * ND * ROWS * COL,
            bytes_accessed=8 * 1024 * 1024,
            transcendentals=0,
        ),
    )(acts, cotangent.reshape(TOK, COL), master, first_moment, second_moment, long_acts)
    outs = pl.pallas_call(
        settle,
        out_shape=out_shape,
        in_specs=[pl.BlockSpec(memory_space=pltpu.VMEM)] * 4,
        out_specs=[anywhere] * 4,
        scratch_shapes=[dma((4,))],
    )(*outs)
    return outs[0], outs[1], outs[2], outs[3].reshape(ROWS, 1, COL)


def solution(mesh):
    in_specs = (
        P("dp", "mp"),
        P("dp", "mp", None),
        P("dp", "mp", None),
        P("dp", "mp", None),
        P("dp", "mp", None),
        P("dp", None),
    )
    out_specs = (
        P(("dp", "mp"), None, None),
        P(("dp", "mp"), None, None),
        P(("dp", "mp"), None, None),
        P("dp", "mp", None),
    )
    return jax.shard_map(
        on_device, mesh=mesh, in_specs=in_specs, out_specs=out_specs, check_vma=False
    )
```

```python
import jax
import jax.numpy as jnp
from jax import lax
from jax.experimental import pallas as pl
from jax.experimental.pallas import tpu as pltpu
from jax.sharding import PartitionSpec as P

beta_one = 0.9
beta_two = 0.95
learn_rate = 0.001
decay_rate = 0.1
adam_eps = 1e-08
steps_done = 100
fix_one = 1.0 - beta_one**steps_done
fix_two = 1.0 - beta_two**steps_done

F32, BF16 = jnp.float32, jnp.bfloat16
NZ = 8
NM = 8
ND = 32
FEAT = 1024
TOK = 1024
COL = 256
HALF = FEAT // 2
CH = HALF // NZ
ROWS = 256


def dp_index(xh, z, k):
    return xh * 16 + z * 2 + k


def mp_index(y, xl):
    return y * 2 + xl


def remote(src, dst, send_sem, recv_sem, dev):
    return pltpu.make_async_remote_copy(
        src_ref=src,
        dst_ref=dst,
        send_sem=send_sem,
        recv_sem=recv_sem,
        device_id=dev,
        device_id_type=pl.DeviceIdType.MESH,
    )


def adamw(master, first, second, grad):
    first_next = beta_one * first + (1.0 - beta_one) * grad
    second_next = beta_two * second + (1.0 - beta_two) * grad * grad
    update = (
        first_next / fix_one / (jnp.sqrt(second_next / fix_two) + adam_eps) + decay_rate * master
    )
    return master - learn_rate * update, first_next, second_next


def kernel(
    acts_hbm, cot_hbm, mas_hbm, fir_hbm, sec_hbm, long_hbm,
    nm_hbm, nf_hbm, ns_hbm, kv_hbm,
    acts_v, acts_t, cots, prod, pair_out, pair_in, ring_out, ring_in, fin, land,
    raw, state, lent, grad_out, grad_in, fresh, arrived, out_v, w_all, long_v, acc, kv_v,
    load_sem, out_sem, cot_send, cot_recv, pair_send, pair_recv, ring_send, ring_recv,
    fin_send, land_recv, pre_send, pre_recv, post_send, post_recv,
    st_send, st_recv, x_send, x_recv, wr_send, wr_recv, sib_send, sib_recv,
):
    d, m = lax.axis_index("dp"), lax.axis_index("mp")
    xh, z, k = d // 16, (d // 2) % NZ, d % 2
    y, xl = m // 2, m % 2
    up, down = (z + 1) % NZ, (z + NZ - 1) % NZ
    yp, ym, yo = (y + 1) % 4, (y + 3) % 4, (y + 2) % 4
    xn = (d, mp_index(y, 1 - xl))
    dev_yp, dev_ym = (d, mp_index(yp, xl)), (d, mp_index(ym, xl))
    sib = (dp_index(xh, z, 1 - k), m)
    dev_up, dev_down = (dp_index(xh, up, k), m), (dp_index(xh, down, k), m)
    xpart = (dp_index(1 - xh, z, k), m)
    dt = dp_index(m // 4, z, k)

    def lender(zi, ki):
        return 4 * (z % 2) + 2 * k + zi, ki

    def owner(q):
        return 2 * q + z // 4, (z // 2) % 2

    loads = [
        pltpu.make_async_copy(cot_hbm, cots.at[m], load_sem.at[0]),
        pltpu.make_async_copy(acts_hbm, acts_v, load_sem.at[1]),
        pltpu.make_async_copy(mas_hbm, raw.at[0], load_sem.at[2]),
        pltpu.make_async_copy(fir_hbm, raw.at[1], load_sem.at[3]),
        pltpu.make_async_copy(sec_hbm, raw.at[2], load_sem.at[4]),
        pltpu.make_async_copy(long_hbm, long_v, load_sem.at[5]),
    ]
    for load in loads[:5]:
        load.start()

    barrier = pltpu.get_barrier_semaphore()

    def greet(dev):
        pl.semaphore_signal(barrier, inc=1, device_id=dev, device_id_type=pl.DeviceIdType.MESH)

    for dev in (sib, dev_up, dev_down, xpart):
        greet(dev)
    for o in range(1, NM):
        greet((d, (m + o) % NM))
    for o in range(NM):
        greet((dt, (m + o) % NM))
    for a in range(2):
        for q in range(4):
            greet((dp_index(a, z, k), 4 * xh + q))
    for zi in range(2):
        for ki in range(2):
            zt, kt = lender(zi, ki)
            greet((dp_index(xh, zt, kt), m))
    for q in range(4):
        zo, ko = owner(q)
        greet((dp_index(xh, zo, ko), m))
    pl.semaphore_wait(barrier, 4 + NM - 1 + NM + 8 + 4 + 4)

    sends = []

    def go(copy):
        copy.start()
        sends.append(copy)
        return copy

    def go_or_keep(here, src, dst, send_sem, recv_sem, dev):
        @pl.when(here)
        def _():
            pltpu.make_async_copy(src, dst, recv_sem).start()

        @pl.when(jnp.logical_not(here))
        def _():
            remote(src, dst, send_sem, recv_sem, dev).start()

    def sent_or_kept(here, src, dst, send_sem, recv_sem, dev):
        @pl.when(jnp.logical_not(here))
        def _():
            remote(src, dst, send_sem, recv_sem, dev).wait_send()

    head = [
        m, mp_index(y, 1 - xl), mp_index(ym, xl), mp_index(yp, xl),
        mp_index(yo, xl), mp_index(ym, 1 - xl), mp_index(yp, 1 - xl), mp_index(yo, 1 - xl),
    ]
    low, high = pl.ds(0, TOK // 2), pl.ds(TOK // 2, TOK // 2)

    def cot_copy(n, block, dev):
        return remote(block, block, cot_send.at[n], cot_recv.at[n], dev)

    def cot_arrived(n, block):
        cot_copy(n, block, xn).wait_recv()

    def product_for_sib(j):
        def tile(i, carry):
            rows = pl.multiple_of((1 - k) * HALF + i * 256, 256)
            pair_out[j, pl.ds(pl.multiple_of(i * 256, 256), 256), :] = jnp.dot(
                acts_t[pl.ds(rows, 256), :], cots[head[j]], preferred_element_type=F32
            ).astype(BF16)
            return carry

        lax.fori_loop(0, HALF // 256, tile, 0)
        go(remote(pair_out.at[j], pair_in.at[j], pair_send.at[j], pair_recv.at[j], sib))

    def product_to_keep(j):
        def tile(i, carry):
            rows = pl.multiple_of(k * HALF + i * 256, 256)
            prod[j, pl.ds(pl.multiple_of(i * 256, 256), 256), :] = jnp.dot(
                acts_t[pl.ds(rows, 256), :], cots[head[j]], preferred_element_type=F32
            )
            return carry

        lax.fori_loop(0, HALF // 256, tile, 0)

    def product(j):
        product_for_sib(j)
        product_to_keep(j)

    def pair_arrived(j):
        remote(pair_out.at[j], pair_in.at[j], pair_send.at[j], pair_recv.at[j], sib).wait_recv()

    def part(s, r):
        return pl.ds(r * CH // 2, CH // 2) if s == 0 else pl.ds(0, CH)

    def ring_copy(j, r, s):
        return remote(
            ring_out.at[j, r, s, part(s, r)], ring_in.at[j, r, s, part(s, r)],
            ring_send.at[j, r, s], ring_recv.at[j, r, s], (dev_up, dev_down)[r],
        )

    def own_part(j, chunk, first, size):
        rows = pl.ds(pl.multiple_of(chunk * CH + first, CH // 2), size)
        return prod[j, rows, :] + pair_in[j, rows, :].astype(F32)

    def ring(j, s):
        for r in range(2):
            chunk = (z + NZ // 2 - s) % NZ if r == 0 else (z + NZ // 2 + s) % NZ
            if s == 0:
                ring_out[j, r, s, part(s, r)] = own_part(
                    j, chunk, r * CH // 2, CH // 2
                ).astype(BF16)
            elif s == 1:
                mine, theirs = part(0, r), part(0, 1 - r)
                ring_out[j, r, s, theirs] = own_part(
                    j, chunk, (1 - r) * CH // 2, CH // 2
                ).astype(BF16)
                total = own_part(j, chunk, r * CH // 2, CH // 2)
                ring_copy(j, r, 0).wait_recv()
                ring_out[j, r, s, mine] = (total + ring_in[j, r, 0, mine].astype(F32)).astype(BF16)
            else:
                total = own_part(j, chunk, 0, CH)
                ring_copy(j, r, s - 1).wait_recv()
                ring_out[j, r, s] = (total + ring_in[j, r, s - 1].astype(F32)).astype(BF16)
            go(ring_copy(j, r, s))

    def finish(j):
        total = own_part(j, z, 0, CH)
        for r in range(2):
            ring_copy(j, r, 3).wait_recv()
            total = total + ring_in[j, r, 3].astype(F32)
        fin[j] = total.astype(BF16)
        hand_over(j)

    def final_args(j):
        slot = (xh, m % 4)
        return (
            dt == d, fin.at[j], land.at[slot], fin_send.at[j], land_recv.at[slot], (dt, head[j])
        )

    def hand_over(j):
        if j > 0:
            go(remote(*final_args(j)[1:]))
        else:
            go_or_keep(*final_args(0))

    place, across = xh * NZ + z, (1 - xh) * NZ + z
    half_rows = pl.ds(pl.multiple_of(k * CH, CH), CH)
    other_rows = pl.ds(pl.multiple_of((1 - k) * CH, CH), CH)
    column = (xl, 1 - xl)

    def view(at, p, u=None, rows=half_rows):
        if u is None:
            return w_all.at[at, :, column[p], rows, :]
        return w_all.at[at, u, column[p], rows, :]

    def units(p, s=0, r=0):
        if s == 3:
            return (r,)
        return (None,) if p == 0 else (0, 1)

    def slot_of(u):
        return 0 if u is None else u

    def x_copy(at, p, u):
        ref = view(at, p, u)
        return remote(ref, ref, x_send.at[p, slot_of(u)], x_recv.at[p, slot_of(u)], xpart)

    def block_of(stream, r, s):
        at = (z + NZ - 1 - s) % NZ if r == 0 else (z + 1 + s) % NZ
        return (xh if stream == 0 else 1 - xh) * NZ + at

    def round_copy(ref, p, stream, r, s, u):
        n = (p, stream, r, s, slot_of(u))
        return remote(ref, ref, wr_send.at[n], wr_recv.at[n], (dev_up, dev_down)[r])

    def send_on(p, stream, r, s, u):
        go(round_copy(view(block_of(stream, r, s - 1), p, u), p, stream, r, s, u))

    def sib_copy(p, n, ref):
        return remote(ref, ref, sib_send.at[p, n], sib_recv.at[p, n], sib)

    def add(at, p):
        value = acc[...]
        for u in range(2):
            source = (at // NZ) * 4 + 2 * u + column[p]
            cols = source * FEAT + (at % NZ) * 2 * CH
            value += jnp.dot(
                long_v[:, pl.ds(pl.multiple_of(cols, 2 * CH), 2 * CH)],
                w_all[at, u, column[p]],
                preferred_element_type=F32,
            )
        acc[...] = value

    pending = []

    def catch_up(entries):
        for p, n, at, u, last in pending:
            sib_copy(p, n, view(at, p, u, other_rows)).wait_recv()
            if last:
                add(at, p)
        pending[:] = entries

    def make_weights(p):
        for u in range(2):
            q = 2 * u + column[p]
            for a in range(2):
                remote(
                    fin.at[0], land.at[a, q], fin_send.at[0], land_recv.at[a, q], xn
                ).wait_recv()
            grad = (land[0, q].astype(F32) + land[1, q].astype(F32)).astype(BF16)
            grad_out[q] = grad
            w_all[place, u, column[p], half_rows, :] = adamw(
                lent[q, 0], lent[q, 1], lent[q, 2], grad.astype(F32)
            )[0].astype(BF16)
        for u in units(p):
            go(x_copy(place, p, u))
            for r in range(2):
                send_on(p, 0, r, 0, u)
        go(sib_copy(p, 0, view(place, p)))

    def crossed(p):
        for u in units(p):
            x_copy(across, p, u).wait_recv()
            for r in range(2):
                send_on(p, 1, r, 0, u)
        go(sib_copy(p, 1, view(across, p)))
        catch_up([(p, 0, place, None, True), (p, 1, across, None, True)])

    def step(p, stream, s):
        come = []
        for r in range(2):
            at = block_of(stream, r, s)
            for u in units(p, s, r):
                round_copy(view(at, p, u), p, stream, r, s, u).wait_recv()
                if s < 2:
                    send_on(p, stream, r, s + 1, u)
                elif s == 2 and (u is None or u == r):
                    send_on(p, stream, r, 3, r)
            n = 2 + stream * 8 + s * 2 + r
            u = None if s < 3 else r
            go(sib_copy(p, n, view(at, p, u)))
            come.append((p, n, at, u, s < 3 or r == 1))
        catch_up(come)

    loads[0].wait()
    def half(j, side):
        return cots.at[head[j], (low, high)[side]]

    go(cot_copy(0, half(0, 0), xn))
    go(cot_copy(2, half(0, 0), dev_yp))
    go(cot_copy(4, half(0, 1), dev_ym))
    go(cot_copy(1, half(0, 1), xn))
    go(cot_copy(3, half(0, 1), dev_yp))
    go(cot_copy(5, half(0, 0), dev_ym))

    def lend_args(zi, ki):
        zt, kt = lender(zi, ki)
        rows = pl.ds(zi * 2 * CH + ki * CH, CH)
        return (
            (zt == z) & (kt == k), state.at[:, rows, :], lent.at[z // 2],
            pre_send.at[2 * zi + ki], pre_recv.at[z // 2], (dp_index(xh, zt, kt), m),
        )

    for n in range(3):
        loads[2 + n].wait()
        state[n] = raw[n, :, 0, :]
    for zi in range(2):
        for ki in range(2):
            go_or_keep(*lend_args(zi, ki))
    loads[5].start()
    loads[1].wait()

    def turn(i, carry):
        block = acts_v[:, pl.ds(pl.multiple_of(i * 2 * CH, 2 * CH), 2 * CH)].T
        at = pl.multiple_of(i * CH, CH)
        acts_t[pl.ds(at, CH), :] = block[:CH]
        acts_t[pl.ds(at + HALF, CH), :] = block[CH:]
        return carry

    lax.fori_loop(0, NZ, turn, 0)
    product(0)
    cot_arrived(2, half(2, 0))
    go(cot_copy(6, half(2, 0), dev_yp))
    cot_arrived(4, half(3, 1))
    go(cot_copy(7, half(3, 1), dev_ym))
    for side in range(2):
        cot_arrived(side, half(1, side))
        go(cot_copy(8 + side, half(1, side), dev_yp))
        go(cot_copy(10 + side, half(1, side), dev_ym))
    product(1)
    cot_arrived(3, half(2, 1))
    product(2)
    cot_arrived(5, half(3, 0))
    product(3)
    for j in range(4):
        pair_arrived(j)
        ring(j, 0)
    cot_arrived(6, half(4, 0))
    go(cot_copy(12, half(4, 0), xn))
    cot_arrived(7, half(4, 1))
    go(cot_copy(13, half(4, 1), xn))
    product(4)
    for j in range(4):
        ring(j, 1)
    pair_arrived(4)
    ring(4, 0)
    for s in range(2, 4):
        for j in range(4):
            ring(j, s)
        ring(4, s - 1)
    for q in range(4):
        remote(
            state.at[:, pl.ds(0, CH), :], lent.at[q], pre_send.at[0], pre_recv.at[q], xn
        ).wait_recv()
    loads[5].wait()
    acc[...] = jnp.zeros_like(acc)
    for j in range(4):
        finish(j)
    ring(4, 3)
    for j in range(5, 8):
        for side in range(2):
            cot_arrived(2 * j - 2 + side, half(j, side))
        product_for_sib(j)
    for j in range(5, 8):
        product_to_keep(j)
        pair_arrived(j)
        ring(j, 0)
    finish(4)
    for j in range(5, 8):
        ring(j, 1)
    make_weights(0)
    for j in range(5, 8):
        ring(j, 2)
    step(0, 0, 0)
    crossed(0)
    for j in range(5, 8):
        ring(j, 3)
    step(0, 0, 1)
    step(0, 1, 0)
    for j in range(5, 8):
        finish(j)
    step(0, 0, 2)
    step(0, 1, 1)
    make_weights(1)

    def post_args(q):
        zo, ko = owner(q)
        slot = 2 * (z % 2) + k
        return (
            (zo == z) & (ko == k), grad_out.at[q], grad_in.at[slot],
            post_send.at[q], post_recv.at[slot], (dp_index(xh, zo, ko), m),
        )

    for q in range(4):
        go_or_keep(*post_args(q))

    def state_copy(o):
        to = (m + o) % NM
        return remote(fresh.at[to], arrived.at[m], st_send.at[o], st_recv.at[o], (d, to))

    outs = [
        pltpu.make_async_copy(out_v.at[n], ref, out_sem.at[n])
        for n, ref in enumerate((nm_hbm, nf_hbm, ns_hbm))
    ]
    step(0, 0, 3)
    step(0, 1, 2)
    step(1, 0, 0)
    crossed(1)
    for n in range(4):
        remote(
            grad_out.at[0], grad_in.at[n], post_send.at[0], post_recv.at[n], xn
        ).wait_recv()
        rows = pl.ds(n * CH, CH)
        new = adamw(
            state[0, rows, :], state[1, rows, :], state[2, rows, :], grad_in[n].astype(F32)
        )
        for a, value in enumerate(new):
            fresh[2 * n, a] = value[: CH // 2]
            fresh[2 * n + 1, a] = value[CH // 2 :]
    for o in range(1, NM):
        go(state_copy(o))
    step(0, 1, 3)
    step(1, 0, 1)
    step(1, 1, 0)
    step(1, 0, 2)
    step(1, 1, 1)
    step(1, 0, 3)
    step(1, 1, 2)
    for a in range(3):
        arrived[m, a] = fresh[m, a]
    for o in range(1, NM):
        at = (m + NM - o) % NM
        remote(fresh.at[m], arrived.at[at], st_send.at[o], st_recv.at[o], xn).wait_recv()
    for a in range(3):
        for h in range(NM):
            out_v[a, :, h, :] = arrived[h, a]
        outs[a].start()
    step(1, 1, 3)
    catch_up([])
    kv_v[...] = acc[...].astype(BF16)
    kv_out = pltpu.make_async_copy(kv_v, kv_hbm, out_sem.at[3])
    kv_out.start()

    for copy in sends:
        copy.wait_send()
    sent_or_kept(*final_args(0))
    for n in range(4):
        sent_or_kept(*lend_args(n // 2, n % 2))
        sent_or_kept(*post_args(n))
    for out in outs:
        out.wait()
    kv_out.wait()


def settle(a_ref, b_ref, c_ref, e_ref, a_hbm, b_hbm, c_hbm, e_hbm, sem):
    pairs = ((a_ref, a_hbm), (b_ref, b_hbm), (c_ref, c_hbm), (e_ref, e_hbm))
    copies = [pltpu.make_async_copy(a, b, sem.at[n]) for n, (a, b) in enumerate(pairs)]
    for copy in copies:
        copy.start()
    for copy in copies:
        copy.wait()


def on_device(acts, cotangent, master, first_moment, second_moment, long_acts):
    state_out = jax.ShapeDtypeStruct((ROWS // NM, NM, COL), F32)
    out_shape = [state_out] * 3 + [jax.ShapeDtypeStruct((ROWS, COL), BF16)]
    dma = pltpu.SemaphoreType.DMA
    anywhere = pl.BlockSpec(memory_space=pl.ANY)
    outs = pl.pallas_call(
        kernel,
        out_shape=out_shape,
        in_specs=[anywhere] * 6,
        out_specs=[anywhere] * 4,
        scratch_shapes=[
            pltpu.VMEM((TOK, FEAT), BF16),
            pltpu.VMEM((FEAT, TOK), BF16),
            pltpu.VMEM((NM, TOK, COL), BF16),
            pltpu.VMEM((NM, HALF, COL), F32),
            pltpu.VMEM((NM, HALF, COL), BF16),
            pltpu.VMEM((NM, HALF, COL), BF16),
            pltpu.VMEM((NM, 2, 4, CH, COL), BF16),
            pltpu.VMEM((NM, 2, 4, CH, COL), BF16),
            pltpu.VMEM((NM, CH, COL), BF16),
            pltpu.VMEM((2, 4, CH, COL), BF16),
            pltpu.VMEM((3, ROWS, 1, COL), F32),
            pltpu.VMEM((3, ROWS, COL), F32),
            pltpu.VMEM((4, 3, CH, COL), F32),
            pltpu.VMEM((4, CH, COL), BF16),
            pltpu.VMEM((4, CH, COL), BF16),
            pltpu.VMEM((NM, 3, ROWS // NM, COL), F32),
            pltpu.VMEM((NM, 3, ROWS // NM, COL), F32),
            pltpu.VMEM((3, ROWS // NM, NM, COL), F32),
            pltpu.VMEM((ND // 2, 2, 2, 2 * CH, COL), BF16),
            pltpu.VMEM((ROWS, ND * ROWS), BF16),
            pltpu.VMEM((ROWS, COL), F32),
            pltpu.VMEM((ROWS, COL), BF16),
            dma((6,)),
            dma((4,)),
            dma((14,)),
            dma((14,)),
            dma((NM,)),
            dma((NM,)),
            dma((NM, 2, 4)),
            dma((NM, 2, 4)),
            dma((NM,)),
            dma((2, 4)),
            dma((4,)),
            dma((4,)),
            dma((4,)),
            dma((4,)),
            dma((NM,)),
            dma((NM,)),
            dma((2, 2)),
            dma((2, 2)),
            dma((2, 2, 2, 4, 2)),
            dma((2, 2, 2, 4, 2)),
            dma((2, 18)),
            dma((2, 18)),
        ],
        compiler_params=pltpu.CompilerParams(
            collective_id=0, has_side_effects=True, vmem_limit_bytes=56 * 1024 * 1024
        ),
        cost_estimate=pl.CostEstimate(
            flops=2 * TOK * FEAT * NM * COL + 2 * ROWS * ND * ROWS * COL,
            bytes_accessed=8 * 1024 * 1024,
            transcendentals=0,
        ),
    )(acts, cotangent.reshape(TOK, COL), master, first_moment, second_moment, long_acts)
    outs = pl.pallas_call(
        settle,
        out_shape=out_shape,
        in_specs=[pl.BlockSpec(memory_space=pltpu.VMEM)] * 4,
        out_specs=[anywhere] * 4,
        scratch_shapes=[dma((4,))],
    )(*outs)
    return outs[0], outs[1], outs[2], outs[3].reshape(ROWS, 1, COL)


def solution(mesh):
    in_specs = (
        P("dp", "mp"),
        P("dp", "mp", None),
        P("dp", "mp", None),
        P("dp", "mp", None),
        P("dp", "mp", None),
        P("dp", None),
    )
    out_specs = (
        P(("dp", "mp"), None, None),
        P(("dp", "mp"), None, None),
        P(("dp", "mp"), None, None),
        P("dp", "mp", None),
    )
    return jax.shard_map(
        on_device, mesh=mesh, in_specs=in_specs, out_specs=out_specs, check_vma=False
    )
```

```python
import jax
import jax.numpy as jnp
from jax import lax
from jax.experimental import pallas as pl
from jax.experimental.pallas import tpu as pltpu
from jax.sharding import PartitionSpec as P

beta_one = 0.9
beta_two = 0.95
learn_rate = 0.001
decay_rate = 0.1
adam_eps = 1e-08
steps_done = 100
fix_one = 1.0 - beta_one**steps_done
fix_two = 1.0 - beta_two**steps_done

F32, BF16 = jnp.float32, jnp.bfloat16
NZ = 8
NM = 8
ND = 32
FEAT = 1024
TOK = 1024
COL = 256
HALF = FEAT // 2
CH = HALF // NZ
ROWS = 256


def dp_index(xh, z, k):
    return xh * 16 + z * 2 + k


def mp_index(y, xl):
    return y * 2 + xl


def remote(src, dst, send_sem, recv_sem, dev):
    return pltpu.make_async_remote_copy(
        src_ref=src,
        dst_ref=dst,
        send_sem=send_sem,
        recv_sem=recv_sem,
        device_id=dev,
        device_id_type=pl.DeviceIdType.MESH,
    )


def adamw(master, first, second, grad):
    first_next = beta_one * first + (1.0 - beta_one) * grad
    second_next = beta_two * second + (1.0 - beta_two) * grad * grad
    update = (
        first_next / fix_one / (jnp.sqrt(second_next / fix_two) + adam_eps) + decay_rate * master
    )
    return master - learn_rate * update, first_next, second_next


def kernel(
    acts_hbm, cot_hbm, mas_hbm, fir_hbm, sec_hbm, long_hbm,
    nm_hbm, nf_hbm, ns_hbm, kv_hbm,
    acts_v, acts_t, cots, prod, pair_out, pair_in, ring_out, ring_in, fin, land,
    raw, state, lent, grad_out, grad_in, fresh, arrived, out_v, w_all, long_v, acc, kv_v,
    load_sem, out_sem, cot_send, cot_recv, pair_send, pair_recv, ring_send, ring_recv,
    fin_send, land_recv, pre_send, pre_recv, post_send, post_recv,
    st_send, st_recv, x_send, x_recv, wr_send, wr_recv, sib_send, sib_recv,
):
    d, m = lax.axis_index("dp"), lax.axis_index("mp")
    xh, z, k = d // 16, (d // 2) % NZ, d % 2
    y, xl = m // 2, m % 2
    up, down = (z + 1) % NZ, (z + NZ - 1) % NZ
    yp, ym, yo = (y + 1) % 4, (y + 3) % 4, (y + 2) % 4
    xn = (d, mp_index(y, 1 - xl))
    dev_yp, dev_ym = (d, mp_index(yp, xl)), (d, mp_index(ym, xl))
    sib = (dp_index(xh, z, 1 - k), m)
    dev_up, dev_down = (dp_index(xh, up, k), m), (dp_index(xh, down, k), m)
    xpart = (dp_index(1 - xh, z, k), m)
    dt = dp_index(m // 4, z, k)

    def lender(zi, ki):
        return 4 * (z % 2) + 2 * k + zi, ki

    def owner(q):
        return 2 * q + z // 4, (z // 2) % 2

    loads = [
        pltpu.make_async_copy(cot_hbm, cots.at[m], load_sem.at[0]),
        pltpu.make_async_copy(acts_hbm, acts_v, load_sem.at[1]),
        pltpu.make_async_copy(mas_hbm, raw.at[0], load_sem.at[2]),
        pltpu.make_async_copy(fir_hbm, raw.at[1], load_sem.at[3]),
        pltpu.make_async_copy(sec_hbm, raw.at[2], load_sem.at[4]),
        pltpu.make_async_copy(long_hbm, long_v, load_sem.at[5]),
    ]
    for load in loads[:5]:
        load.start()

    barrier = pltpu.get_barrier_semaphore()

    def greet(dev):
        pl.semaphore_signal(barrier, inc=1, device_id=dev, device_id_type=pl.DeviceIdType.MESH)

    for dev in (sib, dev_up, dev_down, xpart):
        greet(dev)
    for o in range(1, NM):
        greet((d, (m + o) % NM))
    for o in range(NM):
        greet((dt, (m + o) % NM))
    for a in range(2):
        for q in range(4):
            greet((dp_index(a, z, k), 4 * xh + q))
    for zi in range(2):
        for ki in range(2):
            zt, kt = lender(zi, ki)
            greet((dp_index(xh, zt, kt), m))
    for q in range(4):
        zo, ko = owner(q)
        greet((dp_index(xh, zo, ko), m))
    pl.semaphore_wait(barrier, 4 + NM - 1 + NM + 8 + 4 + 4)

    sends = []

    def go(copy):
        copy.start()
        sends.append(copy)
        return copy

    def go_or_keep(here, src, dst, send_sem, recv_sem, dev):
        @pl.when(here)
        def _():
            pltpu.make_async_copy(src, dst, recv_sem).start()

        @pl.when(jnp.logical_not(here))
        def _():
            remote(src, dst, send_sem, recv_sem, dev).start()

    def sent_or_kept(here, src, dst, send_sem, recv_sem, dev):
        @pl.when(jnp.logical_not(here))
        def _():
            remote(src, dst, send_sem, recv_sem, dev).wait_send()

    head = [
        m, mp_index(y, 1 - xl), mp_index(ym, xl), mp_index(yp, xl),
        mp_index(yo, xl), mp_index(ym, 1 - xl), mp_index(yp, 1 - xl), mp_index(yo, 1 - xl),
    ]
    low, high = pl.ds(0, TOK // 2), pl.ds(TOK // 2, TOK // 2)

    def cot_copy(n, block, dev):
        return remote(block, block, cot_send.at[n], cot_recv.at[n], dev)

    def cot_arrived(n, block):
        cot_copy(n, block, xn).wait_recv()

    def product_for_sib(j):
        def tile(i, carry):
            rows = pl.multiple_of((1 - k) * HALF + i * 256, 256)
            pair_out[j, pl.ds(pl.multiple_of(i * 256, 256), 256), :] = jnp.dot(
                acts_t[pl.ds(rows, 256), :], cots[head[j]], preferred_element_type=F32
            ).astype(BF16)
            return carry

        lax.fori_loop(0, HALF // 256, tile, 0)
        go(remote(pair_out.at[j], pair_in.at[j], pair_send.at[j], pair_recv.at[j], sib))

    def product_to_keep(j):
        def tile(i, carry):
            rows = pl.multiple_of(k * HALF + i * 256, 256)
            prod[j, pl.ds(pl.multiple_of(i * 256, 256), 256), :] = jnp.dot(
                acts_t[pl.ds(rows, 256), :], cots[head[j]], preferred_element_type=F32
            )
            return carry

        lax.fori_loop(0, HALF // 256, tile, 0)

    def product(j):
        product_for_sib(j)
        product_to_keep(j)

    def pair_arrived(j):
        remote(pair_out.at[j], pair_in.at[j], pair_send.at[j], pair_recv.at[j], sib).wait_recv()

    def part(s, r):
        return pl.ds(r * CH // 2, CH // 2) if s == 0 else pl.ds(0, CH)

    def ring_copy(j, r, s):
        return remote(
            ring_out.at[j, r, s, part(s, r)], ring_in.at[j, r, s, part(s, r)],
            ring_send.at[j, r, s], ring_recv.at[j, r, s], (dev_up, dev_down)[r],
        )

    def own_part(j, chunk, first, size):
        rows = pl.ds(pl.multiple_of(chunk * CH + first, CH // 2), size)
        return prod[j, rows, :] + pair_in[j, rows, :].astype(F32)

    def ring(j, s):
        for r in range(2):
            chunk = (z + NZ // 2 - s) % NZ if r == 0 else (z + NZ // 2 + s) % NZ
            if s == 0:
                ring_out[j, r, s, part(s, r)] = own_part(
                    j, chunk, r * CH // 2, CH // 2
                ).astype(BF16)
            elif s == 1:
                mine, theirs = part(0, r), part(0, 1 - r)
                ring_out[j, r, s, theirs] = own_part(
                    j, chunk, (1 - r) * CH // 2, CH // 2
                ).astype(BF16)
                total = own_part(j, chunk, r * CH // 2, CH // 2)
                ring_copy(j, r, 0).wait_recv()
                ring_out[j, r, s, mine] = (total + ring_in[j, r, 0, mine].astype(F32)).astype(BF16)
            else:
                total = own_part(j, chunk, 0, CH)
                ring_copy(j, r, s - 1).wait_recv()
                ring_out[j, r, s] = (total + ring_in[j, r, s - 1].astype(F32)).astype(BF16)
            go(ring_copy(j, r, s))

    def finish(j):
        total = own_part(j, z, 0, CH)
        for r in range(2):
            ring_copy(j, r, 3).wait_recv()
            total = total + ring_in[j, r, 3].astype(F32)
        fin[j] = total.astype(BF16)
        hand_over(j)

    def final_args(j):
        slot = (xh, m % 4)
        return (
            dt == d, fin.at[j], land.at[slot], fin_send.at[j], land_recv.at[slot], (dt, head[j])
        )

    def hand_over(j):
        if j > 0:
            go(remote(*final_args(j)[1:]))
        else:
            go_or_keep(*final_args(0))

    place, across = xh * NZ + z, (1 - xh) * NZ + z
    half_rows = pl.ds(pl.multiple_of(k * CH, CH), CH)
    column = (xl, 1 - xl)

    def put_together(p):
        for u in range(2):
            q = 2 * u + column[p]
            for a in range(2):
                remote(
                    fin.at[0], land.at[a, q], fin_send.at[0], land_recv.at[a, q], xn
                ).wait_recv()
            grad = (land[0, q].astype(F32) + land[1, q].astype(F32)).astype(BF16)
            grad_out[q] = grad
            w_all[place, u, column[p], half_rows, :] = adamw(
                lent[q, 0], lent[q, 1], lent[q, 2], grad.astype(F32)
            )[0].astype(BF16)

    def post_args(q):
        zo, ko = owner(q)
        slot = 2 * (z % 2) + k
        return (
            (zo == z) & (ko == k), grad_out.at[q], grad_in.at[slot],
            post_send.at[q], post_recv.at[slot], (dp_index(xh, zo, ko), m),
        )

    def post(p):
        for u in range(2):
            go_or_keep(*post_args(2 * u + column[p]))

    other_rows = pl.ds(pl.multiple_of((1 - k) * CH, CH), CH)

    def view(at, p, rows=half_rows):
        return w_all.at[at, :, column[p], rows, :]

    def x_copy(at, p):
        return remote(view(at, p), view(at, p), x_send.at[p], x_recv.at[p], xpart)

    def block_of(stream, r, s):
        at = (z + NZ - 1 - s) % NZ if r == 0 else (z + 1 + s) % NZ
        return (xh if stream == 0 else 1 - xh) * NZ + at

    def weights_copy(stream, r, s, p):
        src = view(block_of(stream, r, s - 1), p)
        return remote(
            src, src, wr_send.at[stream, r, s, p], wr_recv.at[stream, r, s, p],
            (dev_up, dev_down)[r],
        )

    def weights_arrived(stream, r, s, p):
        dst = view(block_of(stream, r, s), p)
        remote(
            dst, dst, wr_send.at[stream, r, s, p], wr_recv.at[stream, r, s, p],
            (dev_up, dev_down)[r],
        ).wait_recv()

    def to_sib(n, ref):
        go(remote(ref, ref, sib_send.at[n], sib_recv.at[n], sib))

    def sib_arrived(n, ref):
        remote(ref, ref, sib_send.at[n], sib_recv.at[n], sib).wait_recv()

    loads[0].wait()
    def half(j, side):
        return cots.at[head[j], (low, high)[side]]

    go(cot_copy(0, half(0, 0), xn))
    go(cot_copy(2, half(0, 0), dev_yp))
    go(cot_copy(4, half(0, 1), dev_ym))
    go(cot_copy(1, half(0, 1), xn))
    go(cot_copy(3, half(0, 1), dev_yp))
    go(cot_copy(5, half(0, 0), dev_ym))

    def lend_args(zi, ki):
        zt, kt = lender(zi, ki)
        rows = pl.ds(zi * 2 * CH + ki * CH, CH)
        return (
            (zt == z) & (kt == k), state.at[:, rows, :], lent.at[z // 2],
            pre_send.at[2 * zi + ki], pre_recv.at[z // 2], (dp_index(xh, zt, kt), m),
        )

    for n in range(3):
        loads[2 + n].wait()
        state[n] = raw[n, :, 0, :]
    for zi in range(2):
        for ki in range(2):
            go_or_keep(*lend_args(zi, ki))
    loads[5].start()
    loads[1].wait()

    def turn(i, carry):
        block = acts_v[:, pl.ds(pl.multiple_of(i * 2 * CH, 2 * CH), 2 * CH)].T
        at = pl.multiple_of(i * CH, CH)
        acts_t[pl.ds(at, CH), :] = block[:CH]
        acts_t[pl.ds(at + HALF, CH), :] = block[CH:]
        return carry

    lax.fori_loop(0, NZ, turn, 0)
    product(0)
    cot_arrived(2, half(2, 0))
    go(cot_copy(6, half(2, 0), dev_yp))
    cot_arrived(4, half(3, 1))
    go(cot_copy(7, half(3, 1), dev_ym))
    for side in range(2):
        cot_arrived(side, half(1, side))
        go(cot_copy(8 + side, half(1, side), dev_yp))
        go(cot_copy(10 + side, half(1, side), dev_ym))
    product(1)
    cot_arrived(3, half(2, 1))
    product(2)
    cot_arrived(5, half(3, 0))
    product(3)
    for j in range(4):
        pair_arrived(j)
        ring(j, 0)
    cot_arrived(6, half(4, 0))
    go(cot_copy(12, half(4, 0), xn))
    cot_arrived(7, half(4, 1))
    go(cot_copy(13, half(4, 1), xn))
    product(4)
    for j in range(4):
        ring(j, 1)
    pair_arrived(4)
    ring(4, 0)
    for s in range(2, 4):
        for j in range(4):
            ring(j, s)
        ring(4, s - 1)
    for j in range(5, 8):
        for side in range(2):
            cot_arrived(2 * j - 2 + side, half(j, side))
        product_for_sib(j)
    for j in range(5, 8):
        product_to_keep(j)
    for j in range(5, 8):
        pair_arrived(j)
        ring(j, 0)
    ring(4, 3)
    for j in range(4):
        finish(j)
    for j in range(5, 8):
        ring(j, 1)
    finish(4)
    for s in range(2, 4):
        for j in range(5, 8):
            ring(j, s)
    for q in range(4):
        remote(
            state.at[:, pl.ds(0, CH), :], lent.at[q], pre_send.at[0], pre_recv.at[q], xn
        ).wait_recv()
    put_together(0)
    go(x_copy(place, 0))
    for r in range(2):
        go(weights_copy(0, r, 0, 0))
    post(0)
    for j in range(5, 8):
        finish(j)
    x_copy(across, 0).wait_recv()
    for r in range(2):
        go(weights_copy(1, r, 0, 0))
    put_together(1)
    go(x_copy(place, 1))
    for r in range(2):
        go(weights_copy(0, r, 0, 1))
    for p in range(2):
        to_sib(p, view(place, p))
    to_sib(2, view(across, 0))

    post(1)
    loads[5].wait()

    def add(at, start=False):
        value = 0.0
        for q in range(4):
            cols = ((at // NZ) * 4 + q) * FEAT + (at % NZ) * 2 * CH
            value += jnp.dot(
                long_v[:, pl.ds(pl.multiple_of(cols, 2 * CH), 2 * CH)],
                w_all[at, q // 2, q % 2],
                preferred_element_type=F32,
            )
        if start:
            acc[...] = value
        else:
            acc[...] += value

    def state_copy(o):
        to = (m + o) % NM
        return remote(fresh.at[to], arrived.at[m], st_send.at[o], st_recv.at[o], (d, to))

    outs = [
        pltpu.make_async_copy(out_v.at[n], ref, out_sem.at[n])
        for n, ref in enumerate((nm_hbm, nf_hbm, ns_hbm))
    ]
    pending = [(2, across, 0, False)]

    def catch_up(entries):
        for n, at, p, last in pending:
            sib_arrived(n, view(at, p, other_rows))
            if last:
                add(at)
        pending[:] = entries

    def step(p, stream, s):
        come = []
        for r in range(2) if s < 3 else (p,):
            weights_arrived(stream, r, s, p)
            if s < 2 or (s == 2 and p == r):
                go(weights_copy(stream, r, s + 1, p))
            n = 4 + stream * 16 + s * 4 + r * 2 + p
            at = block_of(stream, r, s)
            to_sib(n, view(at, p))
            come.append((n, at, p, p == 1))
        catch_up(come)

    step(0, 0, 0)
    step(0, 1, 0)
    x_copy(across, 1).wait_recv()
    for r in range(2):
        go(weights_copy(1, r, 0, 1))
    to_sib(3, view(across, 1))
    for p in range(2):
        sib_arrived(p, view(place, p, other_rows))
    add(place, True)
    pending.append((3, across, 1, True))
    step(1, 0, 0)
    step(0, 0, 1)
    step(0, 1, 1)
    step(1, 1, 0)
    for n in range(4):
        remote(
            grad_out.at[0], grad_in.at[n], post_send.at[0], post_recv.at[n], xn
        ).wait_recv()
        rows = pl.ds(n * CH, CH)
        new = adamw(
            state[0, rows, :], state[1, rows, :], state[2, rows, :], grad_in[n].astype(F32)
        )
        for a, value in enumerate(new):
            fresh[2 * n, a] = value[: CH // 2]
            fresh[2 * n + 1, a] = value[CH // 2 :]
    for o in range(1, NM):
        go(state_copy(o))
    step(1, 0, 1)
    step(0, 0, 2)
    step(0, 1, 2)
    step(1, 1, 1)
    step(1, 0, 2)
    step(0, 0, 3)
    step(0, 1, 3)
    step(1, 1, 2)
    for a in range(3):
        arrived[m, a] = fresh[m, a]
    for o in range(1, NM):
        at = (m + NM - o) % NM
        remote(fresh.at[m], arrived.at[at], st_send.at[o], st_recv.at[o], xn).wait_recv()
    for a in range(3):
        for h in range(NM):
            out_v[a, :, h, :] = arrived[h, a]
        outs[a].start()
    step(1, 0, 3)
    step(1, 1, 3)
    catch_up([])
    kv_v[...] = acc[...].astype(BF16)
    kv_out = pltpu.make_async_copy(kv_v, kv_hbm, out_sem.at[3])
    kv_out.start()

    for copy in sends:
        copy.wait_send()
    sent_or_kept(*final_args(0))
    for n in range(4):
        sent_or_kept(*lend_args(n // 2, n % 2))
        sent_or_kept(*post_args(n))
    for out in outs:
        out.wait()
    kv_out.wait()


def settle(a_ref, b_ref, c_ref, e_ref, a_hbm, b_hbm, c_hbm, e_hbm, sem):
    pairs = ((a_ref, a_hbm), (b_ref, b_hbm), (c_ref, c_hbm), (e_ref, e_hbm))
    copies = [pltpu.make_async_copy(a, b, sem.at[n]) for n, (a, b) in enumerate(pairs)]
    for copy in copies:
        copy.start()
    for copy in copies:
        copy.wait()


def on_device(acts, cotangent, master, first_moment, second_moment, long_acts):
    state_out = jax.ShapeDtypeStruct((ROWS // NM, NM, COL), F32)
    out_shape = [state_out] * 3 + [jax.ShapeDtypeStruct((ROWS, COL), BF16)]
    dma = pltpu.SemaphoreType.DMA
    anywhere = pl.BlockSpec(memory_space=pl.ANY)
    outs = pl.pallas_call(
        kernel,
        out_shape=out_shape,
        in_specs=[anywhere] * 6,
        out_specs=[anywhere] * 4,
        scratch_shapes=[
            pltpu.VMEM((TOK, FEAT), BF16),
            pltpu.VMEM((FEAT, TOK), BF16),
            pltpu.VMEM((NM, TOK, COL), BF16),
            pltpu.VMEM((NM, HALF, COL), F32),
            pltpu.VMEM((NM, HALF, COL), BF16),
            pltpu.VMEM((NM, HALF, COL), BF16),
            pltpu.VMEM((NM, 2, 4, CH, COL), BF16),
            pltpu.VMEM((NM, 2, 4, CH, COL), BF16),
            pltpu.VMEM((NM, CH, COL), BF16),
            pltpu.VMEM((2, 4, CH, COL), BF16),
            pltpu.VMEM((3, ROWS, 1, COL), F32),
            pltpu.VMEM((3, ROWS, COL), F32),
            pltpu.VMEM((4, 3, CH, COL), F32),
            pltpu.VMEM((4, CH, COL), BF16),
            pltpu.VMEM((4, CH, COL), BF16),
            pltpu.VMEM((NM, 3, ROWS // NM, COL), F32),
            pltpu.VMEM((NM, 3, ROWS // NM, COL), F32),
            pltpu.VMEM((3, ROWS // NM, NM, COL), F32),
            pltpu.VMEM((ND // 2, 2, 2, 2 * CH, COL), BF16),
            pltpu.VMEM((ROWS, ND * ROWS), BF16),
            pltpu.VMEM((ROWS, COL), F32),
            pltpu.VMEM((ROWS, COL), BF16),
            dma((6,)),
            dma((4,)),
            dma((14,)),
            dma((14,)),
            dma((NM,)),
            dma((NM,)),
            dma((NM, 2, 4)),
            dma((NM, 2, 4)),
            dma((NM,)),
            dma((2, 4)),
            dma((4,)),
            dma((4,)),
            dma((4,)),
            dma((4,)),
            dma((NM,)),
            dma((NM,)),
            dma((2,)),
            dma((2,)),
            dma((2, 2, 4, 2)),
            dma((2, 2, 4, 2)),
            dma((36,)),
            dma((36,)),
        ],
        compiler_params=pltpu.CompilerParams(
            collective_id=0, has_side_effects=True, vmem_limit_bytes=56 * 1024 * 1024
        ),
        cost_estimate=pl.CostEstimate(
            flops=2 * TOK * FEAT * NM * COL + 2 * ROWS * ND * ROWS * COL,
            bytes_accessed=8 * 1024 * 1024,
            transcendentals=0,
        ),
    )(acts, cotangent.reshape(TOK, COL), master, first_moment, second_moment, long_acts)
    outs = pl.pallas_call(
        settle,
        out_shape=out_shape,
        in_specs=[pl.BlockSpec(memory_space=pltpu.VMEM)] * 4,
        out_specs=[anywhere] * 4,
        scratch_shapes=[dma((4,))],
    )(*outs)
    return outs[0], outs[1], outs[2], outs[3].reshape(ROWS, 1, COL)


def solution(mesh):
    in_specs = (
        P("dp", "mp"),
        P("dp", "mp", None),
        P("dp", "mp", None),
        P("dp", "mp", None),
        P("dp", "mp", None),
        P("dp", None),
    )
    out_specs = (
        P(("dp", "mp"), None, None),
        P(("dp", "mp"), None, None),
        P(("dp", "mp"), None, None),
        P("dp", "mp", None),
    )
    return jax.shard_map(
        on_device, mesh=mesh, in_specs=in_specs, out_specs=out_specs, check_vma=False
    )
```
